128 devices in a mesh: ctx: 32 (over x, z, core), head: 4 (over y).
Axes of the slice: x: 4, y: 4, z: 4, core: 2. Of those that a mesh axis runs over, the one named last changes fastest.
Arguments:
- x_in: bfloat16 [32768, 4096], P('ctx', 'head'), may hold values from -6 to 6
- b_in: bfloat16 [32768, 128], P('ctx'), may hold values from -1.796875 to 1.796875
- c_in: bfloat16 [32768, 128], P('ctx'), may hold values from -1.796875 to 1.796875
- d_out: bfloat16 [32768, 4096], P('ctx', 'head'), may hold values from -0.75 to 0.75
- table: float32 [16, 18], replicated, may hold values from 0 to 3, as said below
- level_index: int32 [32768], P('ctx'), may hold values from 0 to 15
Outputs:
- y_out: bfloat16 [32768, 4096], P('ctx', 'head')
- dx_out: bfloat16 [32768, 4096], P('ctx', 'head')
- d_b: float32 [32768, 128], P(('ctx', 'head'))
- d_c: float32 [32768, 128], P(('ctx', 'head'))
The draws below stay inside these ranges and needn't reach their ends.
Inputs may be any that keep to these rules, and one draw needn't show every extreme that they name: `table`: entries are positive.
All inputs are finite; a program needn't handle non-finite values.
Results may differ from the reference program's by a relative error of at most 0.006.
Values sent between devices are 32-bit elements; how exact they have to be, the bound alone decides.
No kernel may reach another device: no remote copies, remote signals or barrier semaphores. Data moves between devices by JAX's collectives and lax.ppermute only.
A program may use at most 128 MiB of HBM per device.

```python
import jax
import jax.numpy as jnp
from jax import lax

HEADS = 64
HEAD_DIM = 64
NSTATE = 128
TOK_DEV = 1024
NTAB = 16
LEVELS = 18
TOKENS = 32768
WIDTH = 4096
N_CTX = 32
N_HEAD = 4


def draw_table(key, part):
    raw_draw = jax.random.uniform(key, (NTAB, LEVELS), jnp.float32)
    row_scale = jnp.exp(jnp.log(0.3) + raw_draw * jnp.log(10.0))
    falloff = jnp.exp2(-0.5 * jnp.arange(LEVELS, dtype=jnp.float32))
    return (row_scale * falloff[None, :]).astype(jnp.float32)


def set_ends(values, stream_key, smallest, high):
    longest = values.shape.index(max(values.shape))
    spots = []
    for shift in (0, 1):
        where = [jax.random.randint(jax.random.fold_in(stream_key, axis), (), 0, length) for axis, length in enumerate(values.shape)]
        where[longest] = (where[longest] + shift) % values.shape[longest]
        spots.append(tuple(where))
    return values.at[spots[0]].set(smallest).at[spots[1]].set(high)


def block_scale(rng, extent, split, low, high):
    loudness = 1.0
    for dim, shards_of in split:
        draws = jax.random.uniform(jax.random.fold_in(jax.random.fold_in(rng, 6), dim), (shards_of,), jnp.float32, low / len(split), high / len(split))
        loudness = loudness * jnp.repeat(jnp.exp(draws), extent[dim] // shards_of).reshape((-1,) + (1,) * (len(extent) - 1 - dim))
    return loudness


def normal_values(rng, extent, width, most, cuts=(), kind=jnp.bfloat16):
    loudness = block_scale(rng, extent, cuts, -0.22, 0.18) if cuts else 1.0
    values = jax.random.normal(rng, extent, jnp.float32) * width * loudness
    return jnp.minimum(jnp.maximum(values, -most), most).astype(kind)


def setup_inputs(seed: int = 0) -> dict:
    key_of = jax.random.split(jax.random.key(seed), 7)
    x_in = normal_values(key_of[0], (TOKENS, WIDTH), 1.0, 6.0, ((0, 32), (1, 4)))
    b_in = normal_values(key_of[1], (TOKENS, NSTATE), 0.3, 1.796875, ((0, 32),))
    c_in = normal_values(key_of[2], (TOKENS, NSTATE), 0.3, 1.796875, ((0, 32),))
    d_out = normal_values(key_of[3], (TOKENS, WIDTH), 0.125, 0.75, ((0, 32), (1, 4)))
    table = draw_table(jax.random.fold_in(key_of[6], 71), 0)
    level_index = set_ends(jax.random.randint(key_of[5], (TOKENS,), 0, NTAB), jax.random.fold_in(key_of[5], 1), 0, NTAB - 1).astype(jnp.int32)
    return dict(x_in=x_in, b_in=b_in, c_in=c_in, d_out=d_out, table=table, level_index=level_index)


def bit_count(values, bits):
    counted = jnp.zeros(values.shape, jnp.int32)
    for digit_no in range(bits):
        counted = counted + (values >= (1 << digit_no)).astype(jnp.int32)
    return counted


def reference(x_in, b_in, c_in, d_out, table, level_index):
    num_blocks = N_CTX
    tok_rows = TOK_DEV
    feat_width = HEADS * HEAD_DIM
    groups_head = N_HEAD
    ctx_bits = num_blocks.bit_length() - 1
    low_bits = tok_rows.bit_length() - 1
    weights_tok = table[level_index]
    xs_block = x_in.reshape(num_blocks, tok_rows, feat_width)
    bs_block = b_in.reshape(num_blocks, tok_rows, NSTATE)
    cs_block = c_in.reshape(num_blocks, tok_rows, NSTATE)
    ds_block = d_out.reshape(num_blocks, tok_rows, feat_width)
    lam_block = weights_tok.reshape(num_blocks, tok_rows, LEVELS)
    state = jnp.einsum("cln,clp->cnp", bs_block.astype(jnp.float32), xs_block.astype(jnp.float32))
    block_ids = jnp.arange(num_blocks, dtype=jnp.int32)
    top_bit = bit_count(block_ids[:, None] ^ block_ids[None, :], ctx_bits) - 1
    level_ids = jnp.arange(ctx_bits, dtype=jnp.int32)
    same_level = top_bit[:, None, :] == level_ids[None, :, None]
    below = (same_level & (block_ids[None, None, :] < block_ids[:, None, None])).astype(jnp.float32)
    above = (same_level & (block_ids[None, None, :] > block_ids[:, None, None])).astype(jnp.float32)
    carry = jnp.einsum("cke,enp->cknp", below, state, precision=lax.Precision.HIGHEST).astype(jnp.bfloat16)
    far_lam = lam_block[:, :, low_bits + 1:low_bits + 1 + ctx_bits]
    rising = (far_lam[:, :, :, None] * cs_block[:, :, None, :].astype(jnp.float32)).astype(jnp.bfloat16)
    grad_state = jnp.einsum("clkn,clp->cknp", rising.astype(jnp.float32), ds_block.astype(jnp.float32))
    back_state = jnp.einsum("cke,eknp->cnp", above, grad_state, precision=lax.Precision.HIGHEST).astype(jnp.bfloat16)
    positions = jnp.arange(tok_rows, dtype=jnp.int32)
    local_level = bit_count(positions[:, None] ^ positions[None, :], low_bits)
    causal = positions[None, :] <= positions[:, None]

    def one_block(bundle):
        x_blk, b_blk, c_blk, d_blk, lam_blk, carry_blk, rise_blk, back_blk = bundle
        weight = jnp.take_along_axis(lam_blk, local_level, axis=1)
        weight = jnp.where(causal, weight, 0.0)
        scores = jnp.dot(c_blk, b_blk.T, preferred_element_type=jnp.float32)
        mixing = (scores * weight).astype(jnp.bfloat16)
        flat_carry = carry_blk.reshape(ctx_bits * NSTATE, feat_width)
        flat_rise = rise_blk.reshape(tok_rows, ctx_bits * NSTATE)
        y_blk = jnp.dot(mixing, x_blk, preferred_element_type=jnp.float32) + jnp.dot(flat_rise, flat_carry, preferred_element_type=jnp.float32)
        dx_blk = jnp.dot(mixing.T, d_blk, preferred_element_type=jnp.float32) + jnp.dot(b_blk, back_blk, preferred_element_type=jnp.float32)
        per_group = jnp.einsum("lgp,mgp->glm", d_blk.reshape(tok_rows, groups_head, -1).astype(jnp.float32), x_blk.reshape(tok_rows, groups_head, -1).astype(jnp.float32))
        d_mix = (per_group * weight[None]).astype(jnp.bfloat16).astype(jnp.float32)
        grad_c = jnp.einsum("glm,mn->ln", d_mix, b_blk.astype(jnp.float32))
        grad_b = jnp.einsum("glm,ln->mn", d_mix, c_blk.astype(jnp.float32))
        far_terms = jnp.dot(d_blk, flat_carry.T, preferred_element_type=jnp.float32).reshape(tok_rows, ctx_bits, NSTATE)
        grad_c = grad_c + jnp.sum(far_terms * lam_blk[:, low_bits + 1:low_bits + 1 + ctx_bits, None], axis=1)
        grad_b = grad_b + jnp.dot(x_blk, back_blk.T, preferred_element_type=jnp.float32)
        return y_blk.astype(jnp.bfloat16), dx_blk.astype(jnp.bfloat16), grad_b, grad_c

    y_all, dx_all, gb_all, gc_all = lax.map(one_block, (xs_block, bs_block, cs_block, ds_block, lam_block, carry, rising, back_state))
    total_rows = num_blocks * tok_rows
    return (y_all.reshape(total_rows, feat_width), dx_all.reshape(total_rows, feat_width), gb_all.reshape(total_rows, NSTATE), gc_all.reshape(total_rows, NSTATE))
```

```python
import jax
import jax.numpy as jnp
from jax import lax
from jax.sharding import PartitionSpec as P


def from_xor(block, flip):
    route = [(i, i ^ flip) for i in range(lax.axis_size("ctx"))]
    return lax.ppermute(block, "ctx", route)


CORE, Z, X = 1, (0, 2, 4, 6), (0, 8, 16, 24)


def sibling_sums(slots):
    a0, a1, a2, a3, a4 = slots
    far = jnp.stack([a3, a4])
    near = jnp.stack([a1, a2])
    far_p = far[:, 0] + from_xor(far[:, 1], CORE)
    near_p = near[:, 0] + from_xor(near[:, 1], CORE)
    b0 = from_xor(a0, CORE)[::-1]
    total = far_p[:, 0]
    for m in (2, 1, 3):
        total = total + from_xor(far_p[:, m], Z[m])
    b3 = from_xor(total[0], X[1])
    b4 = from_xor(total[1], X[2]) + from_xor(total[1], X[3])
    b34 = jnp.stack([b3, b4])
    b1 = from_xor(near_p[0], Z[1])
    b1 = jnp.stack([b1[p ^ 1] for p in range(4)])
    r2, r3 = from_xor(near_p[1], Z[2]), from_xor(near_p[1], Z[3])
    b2 = jnp.stack([r2[p ^ 2] + r3[p ^ 3] for p in range(4)])
    b34_all = jnp.stack([b34] + [from_xor(b34, Z[m]) for m in (1, 2, 3)], axis=1)
    mine = jnp.concatenate([jnp.stack([b1, b2]), b34_all])
    other = from_xor(mine, CORE)
    rest = jnp.stack([mine, other], axis=1)
    return jnp.concatenate([b0[None], rest])


def bit_count(values, bits):
    counted = jnp.zeros(values.shape, jnp.int32)
    for digit_no in range(bits):
        counted = counted + (values >= 1 << digit_no).astype(jnp.int32)
    return counted


def local(x_in, b_in, c_in, d_out, table, level_index):
    tok_rows, feat_width = x_in.shape
    nstate = b_in.shape[1]
    low_bits = tok_rows.bit_length() - 1
    ctx_bits = lax.axis_size("ctx").bit_length() - 1
    my_block = lax.axis_index("ctx")
    mask = ((my_block & 1) << 2 | (my_block >> 1 & 3)) * 16
    iota = jnp.arange(nstate, dtype=jnp.int32)
    perm = (iota[:, None] == (iota[None, :] ^ mask)).astype(jnp.bfloat16)
    chooser = (level_index[:, None] == jnp.arange(table.shape[0], dtype=jnp.int32)[None, :]).astype(jnp.float32)
    weights_tok = jnp.dot(chooser, table, precision=lax.Precision.HIGHEST)
    far_lam = weights_tok[:, low_bits + 1 : low_bits + 1 + ctx_bits]
    b_perm = jnp.dot(b_in, perm, preferred_element_type=jnp.bfloat16)
    c_perm = jnp.dot(c_in, perm, preferred_element_type=jnp.bfloat16)
    state = jnp.dot(b_perm.T, x_in, preferred_element_type=jnp.float32)
    rising = (
        (far_lam[:, :, None] * c_perm[:, None, :].astype(jnp.float32))
        .astype(jnp.bfloat16)
        .reshape(tok_rows, ctx_bits * nstate)
    )
    grad_state = jnp.dot(rising.T, d_out, preferred_element_type=jnp.float32).reshape(ctx_bits, nstate, feat_width)
    bits = [my_block >> k & 1 for k in range(ctx_bits)]
    slots = [jnp.where(bits[k] == 1, grad_state[k], state).reshape(2, 4, 16, feat_width) for k in range(ctx_bits)]
    sums = sibling_sums(slots).reshape(ctx_bits, nstate, feat_width)
    set_bits = jnp.stack(bits).astype(jnp.float32)[:, None, None]
    carry3 = (sums * set_bits).astype(jnp.bfloat16)
    carry = carry3.reshape(ctx_bits * nstate, feat_width)
    back_state = jnp.sum(sums * (1 - set_bits), axis=0).astype(jnp.bfloat16)
    block_rows = min(512, tok_rows)
    positions = jnp.arange(tok_rows, dtype=jnp.int32)
    y_parts = []
    c_parts = []
    dx_accum = jnp.zeros((tok_rows, feat_width), jnp.float32)
    grad_b = jnp.zeros((tok_rows, nstate), jnp.float32)
    for row_start in range(0, tok_rows, block_rows):
        row_stop = row_start + block_rows
        row_pos = positions[row_start:row_stop]
        col_pos = positions[:row_stop]
        level_map = bit_count(row_pos[:, None] ^ col_pos[None, :], low_bits)
        weight = jnp.zeros((block_rows, row_stop), jnp.float32)
        for level_no in range(low_bits + 1):
            weight = weight + jnp.where(level_map == level_no, weights_tok[row_start:row_stop, level_no][:, None], 0.0)
        weight = jnp.where(col_pos[None, :] <= row_pos[:, None], weight, 0.0)
        scores = jnp.dot(c_in[row_start:row_stop], b_in[:row_stop].T, preferred_element_type=jnp.float32)
        mixing = (scores * weight).astype(jnp.bfloat16)
        y_rows = jnp.dot(mixing, x_in[:row_stop], preferred_element_type=jnp.float32) + jnp.dot(
            rising[row_start:row_stop], carry, preferred_element_type=jnp.float32
        )
        y_parts.append(y_rows.astype(jnp.bfloat16))
        dx_accum = dx_accum.at[:row_stop].add(jnp.dot(mixing.T, d_out[row_start:row_stop], preferred_element_type=jnp.float32))
        d_mix = (jnp.dot(d_out[row_start:row_stop], x_in[:row_stop].T, preferred_element_type=jnp.float32) * weight).astype(jnp.bfloat16)
        c_parts.append(jnp.dot(d_mix, b_in[:row_stop], preferred_element_type=jnp.float32))
        grad_b = grad_b.at[:row_stop].add(jnp.dot(d_mix.T, c_in[row_start:row_stop], preferred_element_type=jnp.float32))
    y_out = jnp.concatenate(y_parts, axis=0)
    dx_out = (dx_accum + jnp.dot(b_perm, back_state, preferred_element_type=jnp.float32)).astype(jnp.bfloat16)
    carry_nat = jnp.einsum("ij,kjf->kif", perm, carry3, preferred_element_type=jnp.bfloat16)
    back_nat = jnp.dot(perm, back_state, preferred_element_type=jnp.bfloat16)
    far_terms = jnp.dot(d_out, carry_nat.reshape(ctx_bits * nstate, feat_width).T, preferred_element_type=jnp.float32).reshape(
        tok_rows, ctx_bits, nstate
    )
    grad_c = jnp.concatenate(c_parts, axis=0) + jnp.sum(far_terms * far_lam[:, :, None], axis=1)
    grad_b = grad_b + jnp.dot(x_in, back_nat.T, preferred_element_type=jnp.float32)
    both = jnp.concatenate([grad_b, grad_c], axis=1).reshape(4, tok_rows // 4, 2 * nstate)
    mixed = jnp.sum(lax.all_to_all(both, "head", 0, 0, tiled=True), axis=0)
    return (y_out, dx_out, mixed[:, :nstate], mixed[:, nstate:])


def solution(mesh):
    return jax.shard_map(
        local,
        mesh=mesh,
        in_specs=(P("ctx", "head"), P("ctx", None), P("ctx", None), P("ctx", "head"), P(), P("ctx")),
        out_specs=(P("ctx", "head"), P("ctx", "head"), P(("ctx", "head"), None), P(("ctx", "head"), None)),
        check_vma=False,
    )
```

```python
import jax
import jax.numpy as jnp
from jax import lax
from jax.experimental import pallas as pl
from jax.experimental.pallas import tpu as pltpu
from jax.sharding import PartitionSpec as P

F32, BF16 = jnp.float32, jnp.bfloat16
CORE, Z, X = 1, (0, 2, 4, 6), (0, 8, 16, 24)
TILE = 256
VMEM = pl.BlockSpec(memory_space=pltpu.VMEM)
SMEM = pl.BlockSpec(memory_space=pltpu.SMEM)


def from_xor(block, flip):
    route = [(i, i ^ flip) for i in range(lax.axis_size("ctx"))]
    return lax.ppermute(block, "ctx", route)


def dot_nt(a, b):
    return lax.dot_general(a, b, (((1,), (1,)), ((), ())), preferred_element_type=F32)


def dot_tn(a, b):
    return lax.dot_general(a, b, (((0,), (0,)), ((), ())), preferred_element_type=F32)


def dot_nn(a, b):
    return jnp.dot(a, b, preferred_element_type=F32)


def one_hot(level_ref, rows):
    ids = lax.broadcasted_iota(jnp.int32, (rows, level_ref.shape[1]), 0)
    return (ids == level_ref[...]).astype(F32)


def call(kernel, out_shape, in_specs, flops, scratch=()):
    return pl.pallas_call(
        kernel,
        out_shape=out_shape,
        in_specs=in_specs,
        out_specs=jax.tree.map(lambda _: VMEM, out_shape),
        scratch_shapes=list(scratch),
        compiler_params=pltpu.CompilerParams(vmem_limit_bytes=32 << 20),
        cost_estimate=pl.CostEstimate(flops=flops, bytes_accessed=8 << 20, transcendentals=0),
    )


def own_bits(me):
    return [lax.shift_right_logical(me, k) & 1 for k in range(5)]


def row_mask(me):
    bits = own_bits(me)
    return bits[0] * 64 + bits[2] * 32 + bits[1] * 16


def state_kernel(me_ref, x_ref, b_ref, c_ref, d_ref, table_t_ref, level_ref, a0_ref, near_keep, near_send, far_keep, far_send, left):
    me = me_ref[0]
    bits = own_bits(me)
    n = b_ref.shape[1]
    rows = lax.broadcasted_iota(jnp.int32, (n, n), 0)
    cols = lax.broadcasted_iota(jnp.int32, (n, n), 1)
    perm = (cols == (rows ^ row_mask(me))).astype(F32).astype(BF16)
    c_t = dot_nt(perm, c_ref[...])
    b_t = dot_nt(perm, b_ref[...]).astype(BF16)
    lam_t = jnp.dot(table_t_ref[...], one_hot(level_ref, table_t_ref.shape[1]), precision=lax.Precision.HIGHEST, preferred_element_type=F32)
    for k in range(5):
        left[k * n : (k + 1) * n, :] = (lam_t[11 + k : 12 + k, :] * c_t).astype(BF16)
    half = n // 2
    for at in range(0, x_ref.shape[1], TILE):
        here = slice(at, at + TILE)
        state = dot_nn(b_t, x_ref[:, here])
        grads = dot_nn(left[...], d_ref[:, here])
        for k in range(5):
            value = jnp.where(bits[k] == 1, grads[k * n : (k + 1) * n], state)
            if k == 0:
                a0_ref[:, here] = value
                continue
            keep, send = (near_keep, near_send) if k < 3 else (far_keep, far_send)
            keep[(k - 1) % 2, :, here] = value[:half]
            send[(k - 1) % 2, :, here] = value[half:]


def local_kernel(x_ref, b_ref, c_ref, d_ref, table_ref, level_ref, mix_ref, grad_b_ref, grad_c_ref):
    lam = lax.dot_general(
        one_hot(level_ref, table_ref.shape[0]),
        table_ref[...],
        (((0,), (0,)), ((), ())),
        precision=lax.Precision.HIGHEST,
        preferred_element_type=F32,
    )
    rows = lax.broadcasted_iota(jnp.int32, (TILE, TILE), 0)
    cols = lax.broadcasted_iota(jnp.int32, (TILE, TILE), 1)
    gap = rows ^ cols
    tiles = x_ref.shape[0] // TILE
    for i in range(tiles):
        mine = slice(i * TILE, (i + 1) * TILE)
        lam_i = lam[mine]
        c_i = c_ref[mine, :]
        d_i = d_ref[mine, :]
        grad_c = None
        for j in range(i + 1):
            theirs = slice(j * TILE, (j + 1) * TILE)
            b_j = b_ref[theirs, :]
            if j == i:
                weight = jnp.broadcast_to(lam_i[:, 0:1], (TILE, TILE))
                for level in range(1, 9):
                    weight = jnp.where(gap >= (1 << (level - 1)), lam_i[:, level : level + 1], weight)
                weight = jnp.where(cols <= rows, weight, 0.0)
            else:
                level = 8 + (i ^ j).bit_length()
                weight = lam_i[:, level : level + 1]
            mix_ref[mine, theirs] = (dot_nt(c_i, b_j) * weight).astype(BF16)
            d_mix = (dot_nt(d_i, x_ref[theirs, :]) * weight).astype(BF16)
            term = dot_nn(d_mix, b_j)
            grad_c = term if grad_c is None else grad_c + term
            back = dot_tn(d_mix, c_i)
            if j == i:
                grad_b_ref[theirs, :] = back
            else:
                grad_b_ref[theirs, :] += back
        grad_c_ref[mine, :] = grad_c


def grad_kernel(me_ref, b0_ref, near_ref, near_other, far_ref, far_other, x_ref, d_ref, table_ref, level_ref, gb_ref, gc_ref, both_ref, carry_ref, back_ref):
    me = me_ref[0]
    bits = own_bits(me)
    mask = row_mask(me) // 16
    n = gb_ref.shape[1]
    for p in range(8):
        to = pl.ds(pl.multiple_of((p ^ mask) * 16, 16), 16)
        half, q = p // 4, slice(p % 4 * 16, p % 4 * 16 + 16)
        q0 = slice((p ^ 4) * 16, (p ^ 4) * 16 + 16)
        near, far = (near_ref, far_ref) if half == 0 else (near_other, far_other)
        parts = [b0_ref[q0, :], near[0, q, :], near[1, q, :], far[0, q, :], far[1, q, :]]
        back = None
        for k in range(5):
            carry_ref[k, to, :] = jnp.where(bits[k] == 1, parts[k], 0.0).astype(BF16)
            low = jnp.where(bits[k] == 1, 0.0, parts[k])
            back = low if back is None else back + low
        back_ref[to, :] = back.astype(BF16)
    lam = lax.dot_general(
        one_hot(level_ref, table_ref.shape[0]),
        table_ref[...],
        (((0,), (0,)), ((), ())),
        precision=lax.Precision.HIGHEST,
        preferred_element_type=F32,
    )
    for i in range(x_ref.shape[0] // TILE):
        mine = slice(i * TILE, (i + 1) * TILE)
        d_i = d_ref[mine, :]
        grad_c = gc_ref[mine, :]
        for k in range(5):
            grad_c = grad_c + dot_nt(d_i, carry_ref[k]) * lam[mine, 11 + k : 12 + k]
        both_ref[i, 1] = grad_c
        both_ref[i, 0] = gb_ref[mine, :] + dot_nt(x_ref[mine, :], back_ref[...])


def output_kernel(mix_ref, x_ref, b_ref, c_ref, d_ref, table_ref, level_ref, carry_ref, back_ref, y_ref, dx_ref):
    lam = lax.dot_general(
        one_hot(level_ref, table_ref.shape[0]),
        table_ref[...],
        (((0,), (0,)), ((), ())),
        precision=lax.Precision.HIGHEST,
        preferred_element_type=F32,
    )
    rows = x_ref.shape[0]
    for i in range(rows // TILE):
        mine = slice(i * TILE, (i + 1) * TILE)
        c_i = c_ref[mine, :].astype(F32)
        total = dot_nn(mix_ref[mine, : (i + 1) * TILE], x_ref[: (i + 1) * TILE, :])
        rising = jnp.concatenate([(c_i * lam[mine, 11 + k : 12 + k]).astype(BF16) for k in range(5)], axis=1)
        carry = carry_ref[...].reshape(5 * carry_ref.shape[1], carry_ref.shape[2])
        y_ref[mine, :] = (total + dot_nn(rising, carry)).astype(BF16)
        total = dot_tn(mix_ref[i * TILE :, mine], d_ref[i * TILE :, :])
        dx_ref[mine, :] = (total + dot_nn(b_ref[mine, :], back_ref[...])).astype(BF16)


def sum_kernel(parts_ref, d_b_ref, d_c_ref):
    d_b_ref[...] = parts_ref[0, 0] + parts_ref[1, 0] + parts_ref[2, 0] + parts_ref[3, 0]
    d_c_ref[...] = parts_ref[0, 1] + parts_ref[1, 1] + parts_ref[2, 1] + parts_ref[3, 1]


def local(x_in, b_in, c_in, d_out, table, level_index):
    rows, width = x_in.shape
    n = b_in.shape[1]
    me = lax.axis_index("ctx").reshape(1)
    level = level_index.reshape(1, rows)
    shape = jax.ShapeDtypeStruct
    half = shape((2, n // 2, width), F32)
    a0, near_keep, near_send, far_keep, far_send = call(
        state_kernel,
        (shape((n, width), F32), half, half, half, half),
        [SMEM] + [VMEM] * 6,
        2 * rows * width * n * 6,
        [pltpu.VMEM((5 * n, rows), BF16)],
    )(me, x_in, b_in, c_in, d_out, table.T, level)
    far = (far_keep + from_xor(far_send, CORE)).reshape(2, 4, n // 8, width)
    near = near_keep + from_xor(near_send, CORE)
    b0 = from_xor(a0, CORE)
    total = far[:, 0]
    for m in (2, 1, 3):
        total = total + from_xor(far[:, m], Z[m])
    b3 = from_xor(total[0], X[1])
    b4 = from_xor(total[1], X[2]) + from_xor(total[1], X[3])
    b34 = jnp.stack([b3, b4])
    near = near.reshape(2, 4, n // 8, width)
    r1, r2, r3 = from_xor(near[0], Z[1]), from_xor(near[1], Z[2]), from_xor(near[1], Z[3])
    near = jnp.stack([jnp.stack([r1[p ^ 1] for p in range(4)]), jnp.stack([r2[p ^ 2] + r3[p ^ 3] for p in range(4)])])
    far = jnp.stack([b34] + [from_xor(b34, Z[m]) for m in (1, 2, 3)], axis=1)
    near, far = near.reshape(2, n // 2, width), far.reshape(2, n // 2, width)
    near_other, far_other = from_xor(near, CORE), from_xor(far, CORE)

    mix, grad_b, grad_c = call(
        local_kernel,
        (shape((rows, rows), BF16), shape((rows, n), F32), shape((rows, n), F32)),
        [VMEM] * 6,
        2 * rows * rows * width // 2,
    )(x_in, b_in, c_in, d_out, table, level)
    both, carry, back = call(
        grad_kernel,
        (shape((4, 2, rows // 4, n), F32), shape((5, n, width), BF16), shape((n, width), BF16)),
        [SMEM] + [VMEM] * 11,
        2 * rows * width * n * 6,
    )(me, b0, near, near_other, far, far_other, x_in, d_out, table, level, grad_b, grad_c)
    parts = lax.all_to_all(both, "head", 0, 0, tiled=True)
    y_out, dx_out = call(
        output_kernel,
        (shape((rows, width), BF16), shape((rows, width), BF16)),
        [VMEM] * 9,
        2 * rows * width * n * 6 + 2 * rows * rows * width,
    )(mix, x_in, b_in, c_in, d_out, table, level, carry, back)
    d_b, d_c = call(sum_kernel, (shape((rows // 4, n), F32), shape((rows // 4, n), F32)), [VMEM], rows * n)(parts)
    return (y_out, dx_out, d_b, d_c)


def solution(mesh):
    return jax.shard_map(
        local,
        mesh=mesh,
        in_specs=(P("ctx", "head"), P("ctx", None), P("ctx", None), P("ctx", "head"), P(), P("ctx")),
        out_specs=(P("ctx", "head"), P("ctx", "head"), P(("ctx", "head"), None), P(("ctx", "head"), None)),
        check_vma=False,
    )
```

```python
import jax
import jax.numpy as jnp
from jax import lax
from jax.experimental import pallas as pl
from jax.experimental.pallas import tpu as pltpu
from jax.sharding import PartitionSpec as P

F32, BF16 = jnp.float32, jnp.bfloat16
CORE, Z, X = 1, (0, 2, 4, 6), (0, 8, 16, 24)
TILE = 256
VMEM = pl.BlockSpec(memory_space=pltpu.VMEM)
HBM = pl.BlockSpec(memory_space=pltpu.HBM)
AHEAD = 2
STATE_MIB = 46


def from_xor(block, flip, axis="ctx"):
    route = [(i, i ^ flip) for i in range(lax.axis_size(axis))]
    return lax.ppermute(block, axis, route)


def dot_nt(a, b):
    return lax.dot_general(a, b, (((1,), (1,)), ((), ())), preferred_element_type=F32)


def dot_tn(a, b):
    return lax.dot_general(a, b, (((0,), (0,)), ((), ())), preferred_element_type=F32)


def dot_nn(a, b):
    return jnp.dot(a, b, preferred_element_type=F32)


def one_hot(level_ref, rows):
    ids = lax.broadcasted_iota(jnp.int32, (rows, level_ref.shape[1]), 0)
    return (ids == level_ref[...]).astype(F32)


def call(kernel, outs, in_specs, flops, scratch=(), mib=16):
    return pl.pallas_call(
        kernel,
        out_shape=tuple(jax.ShapeDtypeStruct(shape, dtype) for shape, dtype in outs),
        in_specs=in_specs,
        out_specs=tuple(VMEM for _ in outs),
        scratch_shapes=list(scratch),
        compiler_params=pltpu.CompilerParams(vmem_limit_bytes=mib << 20),
        cost_estimate=pl.CostEstimate(flops=flops, bytes_accessed=1 << 20, transcendentals=0),
    )


def own_bits():
    me = lax.axis_index("ctx")
    return [lax.shift_right_logical(me, k) & 1 for k in range(5)]


def row_mask(bits):
    return bits[0] * 64 + bits[2] * 32 + bits[1] * 16


def level_weights(level_ref, table_ref):
    return lax.dot_general(
        one_hot(level_ref, table_ref.shape[0]),
        table_ref[...],
        (((0,), (0,)), ((), ())),
        precision=lax.Precision.HIGHEST,
        preferred_element_type=F32,
    )


def state_kernel(x_in, b_in, c_in, d_in, table_in, level_in, far_send, far_keep, rest_send, near_keep, x_ref, b_ref, c_ref, d_ref, lam_ref, table_ref, level_ref, left, sems):
    tiles = [slice(at, at + TILE) for at in range(0, x_ref.shape[1], TILE)]
    started = []

    def fetch(pairs):
        copies = [pltpu.make_async_copy(src, dst, sems.at[len(started) + i]) for i, (src, dst) in enumerate(pairs)]
        for copy in copies:
            copy.start()
        started.extend(copies)
        return copies

    small = fetch([(c_in, c_ref), (b_in, b_ref), (table_in, table_ref), (level_in, level_ref)])
    fetch_tile = lambda here: fetch([(d_in.at[:, here], d_ref.at[:, here]), (x_in.at[:, here], x_ref.at[:, here])])
    big = [fetch_tile(here) for here in tiles[:AHEAD]]
    bits = own_bits()
    n = b_ref.shape[1]
    rows = lax.broadcasted_iota(jnp.int32, (n, n), 0)
    cols = lax.broadcasted_iota(jnp.int32, (n, n), 1)
    perm = (cols == (rows ^ row_mask(bits))).astype(F32).astype(BF16)
    for copy in small:
        copy.wait()
    c_t = dot_nt(perm, c_ref[...])
    b_t = dot_nt(perm, b_ref[...]).astype(BF16)
    lam_t = lax.dot_general(
        table_ref[...],
        one_hot(level_ref, table_ref.shape[0]),
        (((0,), (0,)), ((), ())),
        precision=lax.Precision.HIGHEST,
        preferred_element_type=F32,
    )
    lam_ref[...] = level_weights(level_ref, table_ref)
    for k in range(5):
        left[k * n : (k + 1) * n, :] = (lam_t[11 + k : 12 + k, :] * c_t).astype(BF16)
    half = n // 2
    for i, here in enumerate(tiles):
        for copy in big[i]:
            copy.wait()
        if i + AHEAD < len(tiles):
            big.append(fetch_tile(tiles[i + AHEAD]))
        state = dot_nn(b_t, x_ref[:, here])
        grads = dot_nn(left[...], d_ref[:, here])
        for k in range(5):
            value = jnp.where(bits[k] == 1, grads[k * n : (k + 1) * n], state)
            if k == 0:
                rest_send[0, :, here] = value[:half]
                rest_send[1, :, here] = value[half:]
            elif k < 3:
                near_keep[k - 1, :, here] = value[:half]
                rest_send[k + 1, :, here] = value[half:]
            else:
                far_keep[k - 3, :, here] = value[:half]
                far_send[k - 3, :, here] = value[half:]


def local_kernel(x_ref, b_ref, c_ref, d_ref, lam_ref, which, last, outs):
    mix_ref, grad_b_ref, grad_c_ref = outs
    tiles = [slice(at, at + TILE) for at in range(0, x_ref.shape[0], TILE)]
    rows = lax.broadcasted_iota(jnp.int32, (TILE, TILE), 0)
    cols = lax.broadcasted_iota(jnp.int32, (TILE, TILE), 1)
    gap = rows ^ cols
    if last is None:
        first_row = which[0] * TILE
    else:
        first_row = 0
        stop = (which[-1] + 1) * TILE
        grad_b_ref[...] = last[0][...]
        grad_c_ref[stop:, :] = last[1][...]
    for i in which:
        mine = tiles[i]
        lam_i = lam_ref[mine, :]
        c_i = c_ref[mine, :]
        d_i = d_ref[mine, :]
        grad_c = None
        for j in range(i + 1):
            theirs = tiles[j]
            b_j = b_ref[theirs, :]
            if j == i:
                weight = jnp.broadcast_to(lam_i[:, 0:1], (TILE, TILE))
                for level in range(1, 9):
                    weight = jnp.where(gap >= (1 << (level - 1)), lam_i[:, level : level + 1], weight)
                weight = jnp.where(cols <= rows, weight, 0.0)
            else:
                level = 8 + (i ^ j).bit_length()
                weight = lam_i[:, level : level + 1]
            at = slice((i - which[0]) * TILE, (i - which[0] + 1) * TILE)
            mix_ref[at, theirs] = (dot_nt(c_i, b_j) * weight).astype(BF16)
            d_mix = (dot_nt(d_i, x_ref[theirs, :]) * weight).astype(BF16)
            term = dot_nn(d_mix, b_j)
            grad_c = term if grad_c is None else grad_c + term
            back = dot_tn(d_mix, c_i)
            if last is None and i == which[0]:
                grad_b_ref[theirs, :] = back
            else:
                grad_b_ref[theirs, :] += back
        grad_c_ref[i * TILE - first_row : (i + 1) * TILE - first_row, :] = grad_c


def local_last(*refs):
    local_kernel(*refs[:5], (3,), None, refs[5:])


def local_first(last_b, last_c, *refs):
    local_kernel(*refs[:5], (0, 1, 2), (last_b, last_c), refs[5:])


def grad_kernel(rest_ref, near_ref, near_other, far_ref, far_other, gb_ref, gc_ref, x_ref, d_ref, lam_ref, part0, part1, part2, part3, carry_ref, back_ref):
    head = lax.axis_index("head")
    parts = (part0, part1, part2, part3)
    bits = own_bits()
    mask = row_mask(bits) // 16
    n = gb_ref.shape[1]
    for p in range(8):
        to = (p ^ mask) * 16
        half, q = p // 4, slice(p % 4 * 16, p % 4 * 16 + 16)
        near, far = (near_ref, far_ref) if half == 0 else (near_other, far_other)
        sums = [rest_ref[1 - half, q, :], near[0, q, :], near[1, q, :], far[0, q, :], far[1, q, :]]
        back = None
        for k in range(5):
            carry_ref[pl.ds(pl.multiple_of(k * n + to, 16), 16), :] = jnp.where(bits[k] == 1, sums[k], 0.0).astype(BF16)
            low = jnp.where(bits[k] == 1, 0.0, sums[k])
            back = low if back is None else back + low
        back_ref[pl.ds(pl.multiple_of(to, 16), 16), :] = back.astype(BF16)
    for m in (2, 1, 3, 0):
        mine = pl.ds(pl.multiple_of((head ^ m) * TILE, TILE), TILE)
        far_terms = dot_nt(d_ref[mine, :], carry_ref[...])
        lam = lam_ref[mine, :]
        grad_c = gc_ref[mine, :]
        for k in range(5):
            grad_c = grad_c + far_terms[:, k * n : (k + 1) * n] * lam[:, 11 + k : 12 + k]
        parts[m][1] = grad_c
        parts[m][0] = gb_ref[mine, :] + dot_nt(x_ref[mine, :], back_ref[...])


def output_kernel(mix_first, mix_last, x_ref, b_ref, c_ref, d_ref, lam_ref, carry_ref, back_ref, y_ref, dx_ref):
    tiles = [slice(at, at + TILE) for at in range(0, x_ref.shape[0], TILE)]
    count = len(tiles)
    for i, mine in enumerate(tiles):
        lam = lam_ref[mine, :]
        c_i = c_ref[mine, :].astype(F32)
        rising = jnp.concatenate([(c_i * lam[:, 11 + k : 12 + k]).astype(BF16) for k in range(5)], axis=1)
        total = dot_nn(rising, carry_ref[...])
        mix = mix_first[mine, : mine.stop] if i < count - 1 else mix_last[...]
        y_ref[mine, :] = (total + dot_nn(mix, x_ref[: mine.stop, :])).astype(BF16)
    for i, mine in enumerate(tiles):
        total = dot_nn(b_ref[mine, :], back_ref[...]) + dot_tn(mix_last[:, mine], d_ref[tiles[-1], :])
        if i < count - 1:
            total = total + dot_tn(mix_first[mine.start :, mine], d_ref[mine.start : tiles[-1].start, :])
        dx_ref[mine, :] = total.astype(BF16)


def sum_kernel(part0, part1, part2, part3, d_b_ref, d_c_ref):
    d_b_ref[...] = part0[0] + part1[0] + part2[0] + part3[0]
    d_c_ref[...] = part0[1] + part1[1] + part2[1] + part3[1]


def local(x_in, b_in, c_in, d_out, table, level_index):
    rows, width = x_in.shape
    n = b_in.shape[1]
    level = level_index.reshape(1, rows)
    most = rows - TILE
    tie = lax.optimization_barrier
    half = ((2, n // 2, width), F32)
    big, small = ((rows, width), BF16), ((rows, n), BF16)
    far_send, far_keep, rest_send, near_keep, x_in, b_in, c_in, d_out, lam = call(
        state_kernel,
        (half, half, ((4, n // 2, width), F32), half, big, small, small, big, ((rows, table.shape[1]), F32)),
        [HBM] * 6,
        2 * rows * width * n * 6,
        [
            pltpu.VMEM(table.shape, F32),
            pltpu.VMEM((1, rows), jnp.int32),
            pltpu.VMEM((5 * n, rows), BF16),
            pltpu.SemaphoreType.DMA((12,)),
        ],
        STATE_MIB,
    )(x_in, b_in, c_in, d_out, table, level)
    far = (far_keep + from_xor(far_send, CORE)).reshape(2, 4, n // 8, width)
    rest = from_xor(rest_send, CORE)
    near = (near_keep + rest[2:]).reshape(2, 4, n // 8, width)
    taken = [from_xor(far[:, m], Z[m]) for m in (2, 1, 3)]
    local_outs = lambda mix, grad_c_rows: ((mix, BF16), ((rows, n), F32), ((grad_c_rows, n), F32))
    x_tied, far, near = tie((x_in, far, near))
    mix_last, grad_b, grad_c = call(
        local_last,
        local_outs((TILE, rows), TILE),
        [VMEM] * 5,
        rows * rows * width // 2,
    )(x_tied, b_in, c_in, d_out, lam)
    total = far[:, 0]
    for part in taken:
        total = total + part
    total, grad_b = tie((total, grad_b))
    b3 = from_xor(total[0], X[1])
    b4 = from_xor(total[1], X[2]) + from_xor(total[1], X[3])
    b34 = jnp.stack([b3, b4])
    r1, r2, r3 = from_xor(near[0], Z[1]), from_xor(near[1], Z[2]), from_xor(near[1], Z[3])
    gathered = [from_xor(b34, Z[m]) for m in (1, 2, 3)]
    x_tied, b34 = tie((x_in, b34))
    mix_first, grad_b, grad_c = call(
        local_first,
        local_outs((most, most), rows),
        [VMEM] * 7,
        rows * rows * width // 2,
    )(grad_b, grad_c, x_tied, b_in, c_in, d_out, lam)
    r1, r2, r3, gathered, grad_b = tie((r1, r2, r3, gathered, grad_b))
    near = jnp.stack([jnp.stack([r1[p ^ 1] for p in range(4)]), jnp.stack([r2[p ^ 2] + r3[p ^ 3] for p in range(4)])])
    far = jnp.stack([b34] + gathered, axis=1)
    near, far = near.reshape(2, n // 2, width), far.reshape(2, n // 2, width)
    near_other, far_other = from_xor(near, CORE), from_xor(far, CORE)

    piece = ((2, rows // 4, n), F32)
    part0, part1, part2, part3, carry, back = call(
        grad_kernel,
        (piece, piece, piece, piece, ((5 * n, width), BF16), ((n, width), BF16)),
        [VMEM] * 10,
        2 * rows * width * n * 6,
    )(rest, near, near_other, far, far_other, grad_b, grad_c, x_in, d_out, lam)
    part2, part1, part3 = [from_xor(part, m, "head") for part, m in ((part2, 2), (part1, 1), (part3, 3))]
    y_out, dx_out = call(
        output_kernel,
        (((rows, width), BF16), ((rows, width), BF16)),
        [VMEM] * 9,
        2 * rows * width * n * 6 + 2 * rows * rows * width,
    )(mix_first, mix_last, x_in, b_in, c_in, d_out, lam, carry, back)
    piece = ((rows // 4, n), F32)
    d_b, d_c = call(sum_kernel, (piece, piece), [VMEM] * 4, rows * n)(part0, part1, part2, part3)
    return (y_out, dx_out, d_b, d_c)


def solution(mesh):
    return jax.shard_map(
        local,
        mesh=mesh,
        in_specs=(P("ctx", "head"), P("ctx", None), P("ctx", None), P("ctx", "head"), P(), P("ctx")),
        out_specs=(P("ctx", "head"), P("ctx", "head"), P(("ctx", "head"), None), P(("ctx", "head"), None)),
        check_vma=False,
    )
```

```python
import jax
import jax.numpy as jnp
from jax import lax
from jax.experimental import pallas as pl
from jax.experimental.pallas import tpu as pltpu
from jax.sharding import PartitionSpec as P

F32, BF16 = jnp.float32, jnp.bfloat16
CORE, Z, X = 1, (0, 2, 4, 6), (0, 8, 16, 24)
TILE = 256
VMEM = pl.BlockSpec(memory_space=pltpu.VMEM)
LONG = 20 * 10**9


def from_xor(block, flip, axis="ctx"):
    route = [(i, i ^ flip) for i in range(lax.axis_size(axis))]
    return lax.ppermute(block, axis, route)


def dot_nt(a, b):
    return lax.dot_general(a, b, (((1,), (1,)), ((), ())), preferred_element_type=F32)


def dot_tn(a, b):
    return lax.dot_general(a, b, (((0,), (0,)), ((), ())), preferred_element_type=F32)


def dot_nn(a, b):
    return jnp.dot(a, b, preferred_element_type=F32)


def call(kernel, outs, in_specs, flops, scratch=(), mib=16):
    return pl.pallas_call(
        kernel,
        out_shape=tuple(jax.ShapeDtypeStruct(shape, dtype) for shape, dtype in outs),
        in_specs=in_specs,
        out_specs=tuple(VMEM for _ in outs),
        scratch_shapes=list(scratch),
        compiler_params=pltpu.CompilerParams(vmem_limit_bytes=mib << 20),
        cost_estimate=pl.CostEstimate(flops=flops, bytes_accessed=1 << 20, transcendentals=0),
    )


def own_bits():
    me = lax.axis_index("ctx")
    return [lax.shift_right_logical(me, k) & 1 for k in range(5)]


def row_mask(bits):
    return bits[0] * 64 + bits[2] * 32 + bits[1] * 16


def state_kernel(x_ref, bc_ref, d_ref, lam_ref, far_send, far_keep, rest_send, near_keep, left):
    tiles = [slice(at, at + TILE) for at in range(0, x_ref.shape[1], TILE)]
    bits = own_bits()
    n = bc_ref.shape[1] // 2
    rows = lax.broadcasted_iota(jnp.int32, (n, n), 0)
    cols = lax.broadcasted_iota(jnp.int32, (n, n), 1)
    perm = (cols == (rows ^ row_mask(bits))).astype(F32).astype(BF16)
    c_t = dot_nt(perm, bc_ref[:, n:])
    b_t = dot_nt(perm, bc_ref[:, :n]).astype(BF16)
    lam_t = lam_ref[...].T
    for k in range(5):
        left[k * n : (k + 1) * n, :] = (lam_t[11 + k : 12 + k, :] * c_t).astype(BF16)
    half = n // 2
    for here in tiles:
        state = dot_nn(b_t, x_ref[:, here])
        grads = dot_nn(left[...], d_ref[:, here])
        for k in range(5):
            value = jnp.where(bits[k] == 1, grads[k * n : (k + 1) * n], state)
            if k == 0:
                rest_send[0, :, here] = value[:half]
                rest_send[1, :, here] = value[half:]
            elif k < 3:
                near_keep[k - 1, :, here] = value[:half]
                rest_send[k + 1, :, here] = value[half:]
            else:
                far_keep[k - 3, :, here] = value[:half]
                far_send[k - 3, :, here] = value[half:]


def local_kernel(x_ref, b_ref, c_ref, d_ref, lam_ref, which, last, outs):
    mix_ref, grad_b_ref, grad_c_ref = outs
    tiles = [slice(at, at + TILE) for at in range(0, x_ref.shape[0], TILE)]
    rows = lax.broadcasted_iota(jnp.int32, (TILE, TILE), 0)
    cols = lax.broadcasted_iota(jnp.int32, (TILE, TILE), 1)
    gap = rows ^ cols
    if last is None:
        first_row = which[0] * TILE
    else:
        first_row = 0
        stop = (which[-1] + 1) * TILE
        grad_b_ref[...] = last[0][...]
        grad_c_ref[stop:, :] = last[1][...]
    for i in which:
        mine = tiles[i]
        lam_i = lam_ref[mine, :]
        c_i = c_ref[mine, :]
        d_i = d_ref[mine, :]
        grad_c = None
        for j in range(i + 1):
            theirs = tiles[j]
            b_j = b_ref[theirs, :]
            if j == i:
                weight = jnp.broadcast_to(lam_i[:, 0:1], (TILE, TILE))
                for level in range(1, 9):
                    weight = jnp.where(gap >= (1 << (level - 1)), lam_i[:, level : level + 1], weight)
                weight = jnp.where(cols <= rows, weight, 0.0)
            else:
                level = 8 + (i ^ j).bit_length()
                weight = lam_i[:, level : level + 1]
            at = slice((i - which[0]) * TILE, (i - which[0] + 1) * TILE)
            mix_ref[at, theirs] = (dot_nt(c_i, b_j) * weight).astype(BF16)
            d_mix = (dot_nt(d_i, x_ref[theirs, :]) * weight).astype(BF16)
            term = dot_nn(d_mix, b_j)
            grad_c = term if grad_c is None else grad_c + term
            back = dot_tn(d_mix, c_i)
            if last is None and i == which[0]:
                grad_b_ref[theirs, :] = back
            else:
                grad_b_ref[theirs, :] += back
        grad_c_ref[i * TILE - first_row : (i + 1) * TILE - first_row, :] = grad_c


def local_last(*refs):
    local_kernel(*refs[:5], (3,), None, refs[5:])


def local_first(last_b, last_c, *refs):
    local_kernel(*refs[:5], (0, 1, 2), (last_b, last_c), refs[5:])


def shares(m, gb_ref, gc_ref, x_ref, d_ref, lam_ref, carry_ref, back_ref):
    n = gb_ref.shape[1]
    mine = pl.ds(pl.multiple_of((lax.axis_index("head") ^ m) * TILE, TILE), TILE)
    far_terms = dot_nt(d_ref[mine, :], carry_ref[...])
    lam = lam_ref[mine, :]
    grad_c = gc_ref[mine, :]
    for k in range(5):
        grad_c = grad_c + far_terms[:, k * n : (k + 1) * n] * lam[:, 11 + k : 12 + k]
    return gb_ref[mine, :] + dot_nt(x_ref[mine, :], back_ref[...]), grad_c


def grad_kernel(rest_ref, near_ref, near_other, far_ref, far_other, gb_ref, gc_ref, x_ref, d_ref, lam_ref, part2_b, part2_c, carry_ref, back_ref):
    bits = own_bits()
    mask = row_mask(bits) // 16
    n = gb_ref.shape[1]
    for p in range(8):
        to = (p ^ mask) * 16
        half, q = p // 4, slice(p % 4 * 16, p % 4 * 16 + 16)
        near, far = (near_ref, far_ref) if half == 0 else (near_other, far_other)
        sums = [rest_ref[1 - half, q, :], near[0, q, :], near[1, q, :], far[0, q, :], far[1, q, :]]
        back = None
        for k in range(5):
            carry_ref[pl.ds(pl.multiple_of(k * n + to, 16), 16), :] = jnp.where(bits[k] == 1, sums[k], 0.0).astype(BF16)
            low = jnp.where(bits[k] == 1, 0.0, sums[k])
            back = low if back is None else back + low
        back_ref[pl.ds(pl.multiple_of(to, 16), 16), :] = back.astype(BF16)
    part2_b[...], part2_c[...] = shares(2, gb_ref, gc_ref, x_ref, d_ref, lam_ref, carry_ref, back_ref)


def grad_rest_kernel(gb_ref, gc_ref, x_ref, d_ref, lam_ref, carry_ref, back_ref, part0, part1, part3):
    for m, part in ((1, part1), (3, part3), (0, part0)):
        part[0], part[1] = shares(m, gb_ref, gc_ref, x_ref, d_ref, lam_ref, carry_ref, back_ref)


def output_kernel(mix_first, mix_last, x_ref, b_ref, c_ref, d_ref, lam_ref, carry_ref, back_ref, y_ref, dx_ref):
    tiles = [slice(at, at + TILE) for at in range(0, x_ref.shape[0], TILE)]
    count = len(tiles)
    for i, mine in enumerate(tiles):
        lam = lam_ref[mine, :]
        c_i = c_ref[mine, :].astype(F32)
        rising = jnp.concatenate([(c_i * lam[:, 11 + k : 12 + k]).astype(BF16) for k in range(5)], axis=1)
        total = dot_nn(rising, carry_ref[...])
        mix = mix_first[mine, : mine.stop] if i < count - 1 else mix_last[...]
        y_ref[mine, :] = (total + dot_nn(mix, x_ref[: mine.stop, :])).astype(BF16)
    for i, mine in enumerate(tiles):
        total = dot_nn(b_ref[mine, :], back_ref[...]) + dot_tn(mix_last[:, mine], d_ref[tiles[-1], :])
        if i < count - 1:
            total = total + dot_tn(mix_first[mine.start :, mine], d_ref[mine.start : tiles[-1].start, :])
        dx_ref[mine, :] = total.astype(BF16)


def sum_kernel(part0, part1, part3, d_b_ref, d_c_ref):
    d_b_ref[...] = part0[0] + part1[0] + part3[0]
    d_c_ref[...] = part0[1] + part1[1] + part3[1]


def local(x_in, b_in, c_in, d_out, table, level_index):
    rows, width = x_in.shape
    n = b_in.shape[1]
    most = rows - TILE
    tie = lax.optimization_barrier
    half = ((2, n // 2, width), F32)
    table_rows = jnp.arange(table.shape[0], dtype=jnp.int32)
    chooser = (level_index[:, None] == table_rows[None, :]).astype(F32)
    lam = jnp.dot(chooser, table, precision=lax.Precision.HIGHEST)
    far_send, far_keep, rest_send, near_keep = call(
        state_kernel,
        (half, half, ((4, n // 2, width), F32), half),
        [VMEM] * 4,
        2 * rows * width * n * 6,
        [pltpu.VMEM((5 * n, rows), BF16)],
    )(x_in, jnp.concatenate([b_in, c_in], axis=1), d_out, lam)
    far, rest_send = tie((from_xor(far_send, CORE), rest_send))
    far = (far_keep + far).reshape(2, 4, n // 8, width)
    rest = from_xor(rest_send, CORE)
    near = (near_keep + rest[2:]).reshape(2, 4, n // 8, width)
    taken = [from_xor(far[:, m], Z[m]) for m in (2, 1, 3)]
    local_outs = lambda mix, grad_c_rows: ((mix, BF16), ((rows, n), F32), ((grad_c_rows, n), F32))
    x_tied, far, near = tie((x_in, far, near))
    mix_last, grad_b, grad_c = call(
        local_last,
        local_outs((TILE, rows), TILE),
        [VMEM] * 5,
        rows * rows * width // 2,
    )(x_tied, b_in, c_in, d_out, lam)
    total = far[:, 0]
    for part in taken:
        total = total + part
    total, grad_b = tie((total, grad_b))
    b3 = from_xor(total[0], X[1])
    b4 = from_xor(total[1], X[2]) + from_xor(total[1], X[3])
    r1, r2, r3 = from_xor(near[0], Z[1]), from_xor(near[1], Z[2]), from_xor(near[1], Z[3])
    r1, r2, r3, b3, b4 = tie((r1, r2, r3, b3, b4))
    b34 = jnp.stack([b3, b4])
    gathered = [from_xor(b34, Z[m]) for m in (1, 2, 3)]
    near = jnp.stack([jnp.stack([r1[p ^ 1] for p in range(4)]), jnp.stack([r2[p ^ 2] + r3[p ^ 3] for p in range(4)])])
    near = near.reshape(2, n // 2, width)
    near_other = from_xor(near, CORE)
    x_tied, near, near_other = tie((x_in, near, near_other))
    mix_first, grad_b, grad_c = call(
        local_first,
        local_outs((most, most), rows),
        [VMEM] * 7,
        LONG,
    )(grad_b, grad_c, x_tied, b_in, c_in, d_out, lam)
    gathered, grad_b = tie((gathered, grad_b))
    far = jnp.stack([b34] + gathered, axis=1).reshape(2, n // 2, width)
    far_other = from_xor(far, CORE)

    piece = ((2, rows // 4, n), F32)
    part2_b, part2_c, carry, back = call(
        grad_kernel,
        (((rows // 4, n), F32), ((rows // 4, n), F32), ((5 * n, width), BF16), ((n, width), BF16)),
        [VMEM] * 10,
        2 * rows * width * n * 6,
    )(rest, near, near_other, far, far_other, grad_b, grad_c, x_in, d_out, lam)
    part0, part1, part3 = call(
        grad_rest_kernel,
        (piece, piece, piece),
        [VMEM] * 7,
        2 * rows * width * n * 6,
    )(grad_b, grad_c, x_in, d_out, lam, carry, back)
    part3 = part3.at[0].add(from_xor(part2_b, 1, "head"))
    part1 = part1.at[1].add(from_xor(part2_c, 3, "head"))
    part1, part3 = from_xor(part1, 1, "head"), from_xor(part3, 3, "head")
    y_out, dx_out = call(
        output_kernel,
        (((rows, width), BF16), ((rows, width), BF16)),
        [VMEM] * 9,
        2 * rows * width * n * 6 + 2 * rows * rows * width,
    )(mix_first, mix_last, x_in, b_in, c_in, d_out, lam, carry, back)
    piece = ((rows // 4, n), F32)
    d_b, d_c = call(sum_kernel, (piece, piece), [VMEM] * 3, rows * n)(part0, part1, part3)
    return (y_out, dx_out, d_b, d_c)


def solution(mesh):
    return jax.shard_map(
        local,
        mesh=mesh,
        in_specs=(P("ctx", "head"), P("ctx", None), P("ctx", None), P("ctx", "head"), P(), P("ctx")),
        out_specs=(P("ctx", "head"), P("ctx", "head"), P(("ctx", "head"), None), P(("ctx", "head"), None)),
        check_vma=False,
    )
```

```python
import jax
import jax.numpy as jnp
from jax import lax
from jax.experimental import pallas as pl
from jax.experimental.pallas import tpu as pltpu
from jax.sharding import PartitionSpec as P

F32, BF16 = jnp.float32, jnp.bfloat16
CORE, Z, X = 1, (0, 2, 4, 6), (0, 8, 16, 24)
TILE = 256
VMEM = pl.BlockSpec(memory_space=pltpu.VMEM)
FIRST, LAST, LONG = 10**9, 10**9, 20 * 10**9


def from_xor(block, flip, axis="ctx"):
    route = [(i, i ^ flip) for i in range(lax.axis_size(axis))]
    return lax.ppermute(block, axis, route)


def dot_nt(a, b):
    return lax.dot_general(a, b, (((1,), (1,)), ((), ())), preferred_element_type=F32)


def dot_tn(a, b):
    return lax.dot_general(a, b, (((0,), (0,)), ((), ())), preferred_element_type=F32)


def dot_nn(a, b):
    return jnp.dot(a, b, preferred_element_type=F32)


def call(kernel, outs, in_specs, flops, scratch=(), mib=16):
    return pl.pallas_call(
        kernel,
        out_shape=tuple(jax.ShapeDtypeStruct(shape, dtype) for shape, dtype in outs),
        in_specs=in_specs,
        out_specs=tuple(VMEM for _ in outs),
        scratch_shapes=list(scratch),
        compiler_params=pltpu.CompilerParams(vmem_limit_bytes=mib << 20),
        cost_estimate=pl.CostEstimate(flops=flops, bytes_accessed=1 << 20, transcendentals=0),
    )


def own_bits():
    me = lax.axis_index("ctx")
    return [lax.shift_right_logical(me, k) & 1 for k in range(5)]


def row_mask(bits):
    return bits[0] * 64 + bits[2] * 32 + bits[1] * 16


def state_kernel(x_ref, bc_ref, d_ref, lam_ref, far_send, far_keep, rest_send, near_keep, left):
    tiles = [slice(at, at + TILE) for at in range(0, x_ref.shape[1], TILE)]
    bits = own_bits()
    n = bc_ref.shape[1] // 2
    rows = lax.broadcasted_iota(jnp.int32, (n, n), 0)
    cols = lax.broadcasted_iota(jnp.int32, (n, n), 1)
    perm = (cols == (rows ^ row_mask(bits))).astype(F32).astype(BF16)
    c_t = dot_nt(perm, bc_ref[:, n:])
    b_t = dot_nt(perm, bc_ref[:, :n]).astype(BF16)
    lam_t = lam_ref[...].T
    for k in range(5):
        left[k * n : (k + 1) * n, :] = (lam_t[11 + k : 12 + k, :] * c_t).astype(BF16)
    half = n // 2
    for here in tiles:
        state = dot_nn(b_t, x_ref[:, here])
        grads = dot_nn(left[...], d_ref[:, here])
        for k in range(5):
            value = jnp.where(bits[k] == 1, grads[k * n : (k + 1) * n], state)
            if k == 0:
                rest_send[0, :, here] = value[:half]
                rest_send[1, :, here] = value[half:]
            elif k < 3:
                near_keep[k - 1, :, here] = value[:half]
                rest_send[k + 1, :, here] = value[half:]
            else:
                far_keep[k - 3, :, here] = value[:half]
                far_send[k - 3, :, here] = value[half:]


def local_kernel(x_ref, b_ref, c_ref, d_ref, lam_ref, which, last, outs):
    mix_ref, grad_b_ref, grad_c_ref = outs
    tiles = [slice(at, at + TILE) for at in range(0, x_ref.shape[0], TILE)]
    rows = lax.broadcasted_iota(jnp.int32, (TILE, TILE), 0)
    cols = lax.broadcasted_iota(jnp.int32, (TILE, TILE), 1)
    gap = rows ^ cols
    if last is None:
        grad_b_ref[...] = jnp.zeros(grad_b_ref.shape, F32)
        grad_c_ref[...] = jnp.zeros(grad_c_ref.shape, F32)
    else:
        grad_b_ref[...] = last[0][...]
        grad_c_ref[...] = last[1][...]
    for i in which:
        mine = tiles[i]
        lam_i = lam_ref[mine, :]
        c_i = c_ref[mine, :]
        d_i = d_ref[mine, :]
        grad_c = None
        for j in range(i + 1):
            theirs = tiles[j]
            b_j = b_ref[theirs, :]
            if j == i:
                weight = jnp.broadcast_to(lam_i[:, 0:1], (TILE, TILE))
                for level in range(1, 9):
                    weight = jnp.where(gap >= (1 << (level - 1)), lam_i[:, level : level + 1], weight)
                weight = jnp.where(cols <= rows, weight, 0.0)
            else:
                level = 8 + (i ^ j).bit_length()
                weight = lam_i[:, level : level + 1]
            at = slice((i - which[0]) * TILE, (i - which[0] + 1) * TILE)
            mix_ref[at, theirs] = (dot_nt(c_i, b_j) * weight).astype(BF16)
            d_mix = (dot_nt(d_i, x_ref[theirs, :]) * weight).astype(BF16)
            term = dot_nn(d_mix, b_j)
            grad_c = term if grad_c is None else grad_c + term
            back = dot_tn(d_mix, c_i)
            grad_b_ref[theirs, :] += back
        grad_c_ref[mine, :] = grad_c


def local_first(*refs):
    local_kernel(*refs[:5], (0,), None, refs[5:])


def local_last(last_b, last_c, *refs):
    local_kernel(*refs[:5], (3,), (last_b, last_c), refs[5:])


def local_middle(last_b, last_c, *refs):
    local_kernel(*refs[:5], (1, 2), (last_b, last_c), refs[5:])


def shares(m, gb_ref, gc_ref, x_ref, d_ref, lam_ref, carry_ref, back_ref):
    n = gb_ref.shape[1]
    mine = pl.ds(pl.multiple_of((lax.axis_index("head") ^ m) * TILE, TILE), TILE)
    far_terms = dot_nt(d_ref[mine, :], carry_ref[...])
    lam = lam_ref[mine, :]
    grad_c = gc_ref[mine, :]
    for k in range(5):
        grad_c = grad_c + far_terms[:, k * n : (k + 1) * n] * lam[:, 11 + k : 12 + k]
    return gb_ref[mine, :] + dot_nt(x_ref[mine, :], back_ref[...]), grad_c


def grad_kernel(rest_ref, near_ref, near_other, far_ref, far_other, gb_ref, gc_ref, x_ref, d_ref, lam_ref, part2_b, part2_c, carry_ref, back_ref):
    bits = own_bits()
    mask = row_mask(bits) // 16
    n = gb_ref.shape[1]
    for p in range(8):
        to = (p ^ mask) * 16
        half, q = p // 4, slice(p % 4 * 16, p % 4 * 16 + 16)
        near, far = (near_ref, far_ref) if half == 0 else (near_other, far_other)
        sums = [rest_ref[1 - half, q, :], near[0, q, :], near[1, q, :], far[0, q, :], far[1, q, :]]
        back = None
        for k in range(5):
            carry_ref[pl.ds(pl.multiple_of(k * n + to, 16), 16), :] = jnp.where(bits[k] == 1, sums[k], 0.0).astype(BF16)
            low = jnp.where(bits[k] == 1, 0.0, sums[k])
            back = low if back is None else back + low
        back_ref[pl.ds(pl.multiple_of(to, 16), 16), :] = back.astype(BF16)
    part2_b[...], part2_c[...] = shares(2, gb_ref, gc_ref, x_ref, d_ref, lam_ref, carry_ref, back_ref)


def grad_rest_kernel(gb_ref, gc_ref, x_ref, d_ref, lam_ref, carry_ref, back_ref, part0, part1, part3):
    for m, part in ((1, part1), (3, part3), (0, part0)):
        part[0], part[1] = shares(m, gb_ref, gc_ref, x_ref, d_ref, lam_ref, carry_ref, back_ref)


def output_kernel(mix_first, mix_middle, mix_last, x_ref, b_ref, c_ref, d_ref, lam_ref, carry_ref, back_ref, y_ref, dx_ref):
    tiles = [slice(at, at + TILE) for at in range(0, x_ref.shape[0], TILE)]
    mixes = {0: mix_first[...], 1: mix_middle[:TILE, : 2 * TILE], 2: mix_middle[TILE:, :], 3: mix_last[...]}
    for i, mine in enumerate(tiles):
        lam = lam_ref[mine, :]
        c_i = c_ref[mine, :].astype(F32)
        rising = jnp.concatenate([(c_i * lam[:, 11 + k : 12 + k]).astype(BF16) for k in range(5)], axis=1)
        total = dot_nn(rising, carry_ref[...])
        y_ref[mine, :] = (total + dot_nn(mixes[i], x_ref[: mine.stop, :])).astype(BF16)
    middle = slice(TILE, 3 * TILE)
    for i, mine in enumerate(tiles):
        total = dot_nn(b_ref[mine, :], back_ref[...]) + dot_tn(mix_last[:, mine], d_ref[tiles[3], :])
        if i < 2:
            total = total + dot_tn(mix_middle[:, mine], d_ref[middle, :])
        if i == 2:
            total = total + dot_tn(mix_middle[TILE:, mine], d_ref[mine, :])
        if i == 0:
            total = total + dot_tn(mix_first[...], d_ref[mine, :])
        dx_ref[mine, :] = total.astype(BF16)


def sum_kernel(part0, part1, part3, d_b_ref, d_c_ref):
    d_b_ref[...] = part0[0] + part1[0] + part3[0]
    d_c_ref[...] = part0[1] + part1[1] + part3[1]


def local(x_in, b_in, c_in, d_out, table, level_index):
    rows, width = x_in.shape
    n = b_in.shape[1]
    tie = lax.optimization_barrier
    half = ((2, n // 2, width), F32)
    table_rows = jnp.arange(table.shape[0], dtype=jnp.int32)
    chooser = (level_index[:, None] == table_rows[None, :]).astype(F32)
    lam = jnp.dot(chooser, table, precision=lax.Precision.HIGHEST)
    far_send, far_keep, rest_send, near_keep = call(
        state_kernel,
        (half, half, ((4, n // 2, width), F32), half),
        [VMEM] * 4,
        2 * rows * width * n * 6,
        [pltpu.VMEM((5 * n, rows), BF16)],
    )(x_in, jnp.concatenate([b_in, c_in], axis=1), d_out, lam)
    far, rest_send = tie((from_xor(far_send, CORE), rest_send))
    far = (far_keep + far).reshape(2, 4, n // 8, width)
    rest = from_xor(rest_send, CORE)
    near = (near_keep + rest[2:]).reshape(2, 4, n // 8, width)
    taken = [from_xor(far[:, m], Z[m]) for m in (2, 1, 3)]
    def local_part(kernel, mix, operands, flops):
        return call(kernel, ((mix, BF16), ((rows, n), F32), ((rows, n), F32)), [VMEM] * len(operands), flops)(*operands)

    x_tied, far, near = tie((x_in, far, near))
    mix_first, grad_b, grad_c = local_part(local_first, (TILE, TILE), (x_tied, b_in, c_in, d_out, lam), FIRST)
    total = far[:, 0]
    for part in taken:
        total = total + part
    total, grad_b = tie((total, grad_b))
    b3 = from_xor(total[0], X[1])
    b4 = from_xor(total[1], X[2]) + from_xor(total[1], X[3])
    r1, r3 = from_xor(near[0], Z[1]), from_xor(near[1], Z[3])
    x_tied, _ = tie((x_in, total))
    mix_last, grad_b, grad_c = local_part(local_last, (TILE, rows), (grad_b, grad_c, x_tied, b_in, c_in, d_out, lam), LAST)
    r1, r3, b3, b4, grad_b = tie((r1, r3, b3, b4, grad_b))
    b34 = jnp.stack([b3, b4])
    gathered = [from_xor(b34, Z[m]) for m in (1, 2, 3)]
    r2 = from_xor(r3, Z[1])
    x_tied, b34 = tie((x_in, b34))
    mix_middle, grad_b, grad_c = local_part(
        local_middle, (2 * TILE, 3 * TILE), (grad_b, grad_c, x_tied, b_in, c_in, d_out, lam), LONG
    )
    near = jnp.stack([jnp.stack([r1[p ^ 1] for p in range(4)]), jnp.stack([r2[p ^ 2] + r3[p ^ 3] for p in range(4)])])
    near = near.reshape(2, n // 2, width)
    gathered, near, grad_b = tie((gathered, near, grad_b))
    far = jnp.stack([b34] + gathered, axis=1).reshape(2, n // 2, width)
    far_other, near_other = from_xor(far, CORE), from_xor(near, CORE)

    piece = ((2, rows // 4, n), F32)
    part2_b, part2_c, carry, back = call(
        grad_kernel,
        (((rows // 4, n), F32), ((rows // 4, n), F32), ((5 * n, width), BF16), ((n, width), BF16)),
        [VMEM] * 10,
        2 * rows * width * n * 6,
    )(rest, near, near_other, far, far_other, grad_b, grad_c, x_in, d_out, lam)
    part0, part1, part3 = call(
        grad_rest_kernel,
        (piece, piece, piece),
        [VMEM] * 7,
        2 * rows * width * n * 6,
    )(grad_b, grad_c, x_in, d_out, lam, carry, back)
    part3 = part3.at[0].add(from_xor(part2_b, 1, "head"))
    part1 = part1.at[1].add(from_xor(part2_c, 3, "head"))
    part1, part3 = from_xor(part1, 1, "head"), from_xor(part3, 3, "head")
    y_out, dx_out = call(
        output_kernel,
        (((rows, width), BF16), ((rows, width), BF16)),
        [VMEM] * 10,
        2 * rows * width * n * 6 + 2 * rows * rows * width,
    )(mix_first, mix_middle, mix_last, x_in, b_in, c_in, d_out, lam, carry, back)
    piece = ((rows // 4, n), F32)
    d_b, d_c = call(sum_kernel, (piece, piece), [VMEM] * 3, rows * n)(part0, part1, part3)
    return (y_out, dx_out, d_b, d_c)


def solution(mesh):
    return jax.shard_map(
        local,
        mesh=mesh,
        in_specs=(P("ctx", "head"), P("ctx", None), P("ctx", None), P("ctx", "head"), P(), P("ctx")),
        out_specs=(P("ctx", "head"), P("ctx", "head"), P(("ctx", "head"), None), P(("ctx", "head"), None)),
        check_vma=False,
    )
```

```python
import jax
import jax.numpy as jnp
from jax import lax
from jax.experimental import pallas as pl
from jax.experimental.pallas import tpu as pltpu
from jax.sharding import PartitionSpec as P

F32, BF16 = jnp.float32, jnp.bfloat16
CORE, Z, X = 1, (0, 2, 4, 6), (0, 8, 16, 24)
TILE = 256
VMEM = pl.BlockSpec(memory_space=pltpu.VMEM)
FIRST, LAST, LONG = 10**9, 10**9, 20 * 10**9


def from_xor(block, flip, axis="ctx"):
    route = [(i, i ^ flip) for i in range(lax.axis_size(axis))]
    return lax.ppermute(block, axis, route)


def dot_nt(a, b):
    return lax.dot_general(a, b, (((1,), (1,)), ((), ())), preferred_element_type=F32)


def dot_tn(a, b):
    return lax.dot_general(a, b, (((0,), (0,)), ((), ())), preferred_element_type=F32)


def dot_nn(a, b):
    return jnp.dot(a, b, preferred_element_type=F32)


def call(kernel, outs, in_specs, flops, scratch=(), mib=16):
    return pl.pallas_call(
        kernel,
        out_shape=tuple(jax.ShapeDtypeStruct(shape, dtype) for shape, dtype in outs),
        in_specs=in_specs,
        out_specs=tuple(VMEM for _ in outs),
        scratch_shapes=list(scratch),
        compiler_params=pltpu.CompilerParams(vmem_limit_bytes=mib << 20),
        cost_estimate=pl.CostEstimate(flops=flops, bytes_accessed=1 << 20, transcendentals=0),
    )


def own_bits():
    me = lax.axis_index("ctx")
    return [lax.shift_right_logical(me, k) & 1 for k in range(5)]


def row_mask(bits):
    return bits[0] * 64 + bits[2] * 32 + bits[1] * 16


def rows_kernel(bc_ref, lam_ref, b_t_ref, left):
    bits = own_bits()
    n = bc_ref.shape[1] // 2
    rows = lax.broadcasted_iota(jnp.int32, (n, n), 0)
    cols = lax.broadcasted_iota(jnp.int32, (n, n), 1)
    perm = (cols == (rows ^ row_mask(bits))).astype(F32).astype(BF16)
    c_t = dot_nt(perm, bc_ref[:, n:])
    b_t_ref[...] = dot_nt(perm, bc_ref[:, :n]).astype(BF16)
    lam_t = lam_ref[...].T
    for k in range(5):
        left[k * n : (k + 1) * n, :] = (lam_t[11 + k : 12 + k, :] * c_t).astype(BF16)


def state_kernel(x_ref, d_ref, b_t_ref, left, far_send, far_keep, rest_send, near_keep):
    bits = own_bits()
    n = b_t_ref.shape[0]
    half = n // 2
    for at in range(0, x_ref.shape[1], TILE):
        here = slice(at, at + TILE)
        state = dot_nn(b_t_ref[...], x_ref[:, here])
        grads = dot_nn(left[...], d_ref[:, here])
        for k in range(5):
            value = jnp.where(bits[k] == 1, grads[k * n : (k + 1) * n], state)
            if k == 0:
                rest_send[0, :, here] = value[:half]
                rest_send[1, :, here] = value[half:]
            elif k < 3:
                near_keep[k - 1, :, here] = value[:half]
                rest_send[k + 1, :, here] = value[half:]
            else:
                far_keep[k - 3, :, here] = value[:half]
                far_send[k - 3, :, here] = value[half:]


def local_kernel(x_ref, b_ref, c_ref, d_ref, lam_ref, which, last, outs):
    mix_ref, grad_b_ref, grad_c_ref = outs
    tiles = [slice(at, at + TILE) for at in range(0, x_ref.shape[0], TILE)]
    rows = lax.broadcasted_iota(jnp.int32, (TILE, TILE), 0)
    cols = lax.broadcasted_iota(jnp.int32, (TILE, TILE), 1)
    gap = rows ^ cols
    if last is None:
        grad_b_ref[...] = jnp.zeros(grad_b_ref.shape, F32)
        grad_c_ref[...] = jnp.zeros(grad_c_ref.shape, F32)
    else:
        grad_b_ref[...] = last[0][...]
        grad_c_ref[...] = last[1][...]
    for i in which:
        mine = tiles[i]
        lam_i = lam_ref[mine, :]
        c_i = c_ref[mine, :]
        d_i = d_ref[mine, :]
        grad_c = None
        for j in range(i + 1):
            theirs = tiles[j]
            b_j = b_ref[theirs, :]
            if j == i:
                weight = jnp.broadcast_to(lam_i[:, 0:1], (TILE, TILE))
                for level in range(1, 9):
                    weight = jnp.where(gap >= (1 << (level - 1)), lam_i[:, level : level + 1], weight)
                weight = jnp.where(cols <= rows, weight, 0.0)
            else:
                level = 8 + (i ^ j).bit_length()
                weight = lam_i[:, level : level + 1]
            at = slice((i - which[0]) * TILE, (i - which[0] + 1) * TILE)
            mix_ref[at, theirs] = (dot_nt(c_i, b_j) * weight).astype(BF16)
            d_mix = (dot_nt(d_i, x_ref[theirs, :]) * weight).astype(BF16)
            term = dot_nn(d_mix, b_j)
            grad_c = term if grad_c is None else grad_c + term
            back = dot_tn(d_mix, c_i)
            grad_b_ref[theirs, :] += back
        grad_c_ref[mine, :] = grad_c


def local_first(*refs):
    local_kernel(*refs[:5], (0,), None, refs[5:])


def local_last(last_b, last_c, *refs):
    local_kernel(*refs[:5], (3,), (last_b, last_c), refs[5:])


def local_middle(last_b, last_c, *refs):
    local_kernel(*refs[:5], (1, 2), (last_b, last_c), refs[5:])


def shares(m, gb_ref, gc_ref, x_ref, d_ref, lam_ref, carry_ref, back_ref):
    n = gb_ref.shape[1]
    mine = pl.ds(pl.multiple_of((lax.axis_index("head") ^ m) * TILE, TILE), TILE)
    far_terms = dot_nt(d_ref[mine, :], carry_ref[...])
    lam = lam_ref[mine, :]
    grad_c = gc_ref[mine, :]
    for k in range(5):
        grad_c = grad_c + far_terms[:, k * n : (k + 1) * n] * lam[:, 11 + k : 12 + k]
    return gb_ref[mine, :] + dot_nt(x_ref[mine, :], back_ref[...]), grad_c


def grad_kernel(rest_ref, near_ref, near_other, far_ref, far_other, gb_ref, gc_ref, x_ref, d_ref, lam_ref, part2_b, part2_c, carry_ref, back_ref):
    bits = own_bits()
    mask = row_mask(bits) // 16
    n = gb_ref.shape[1]
    for p in range(8):
        to = (p ^ mask) * 16
        half, q = p // 4, slice(p % 4 * 16, p % 4 * 16 + 16)
        near, far = (near_ref, far_ref) if half == 0 else (near_other, far_other)
        sums = [rest_ref[1 - half, q, :], near[0, q, :], near[1, q, :], far[0, q, :], far[1, q, :]]
        back = None
        for k in range(5):
            carry_ref[pl.ds(pl.multiple_of(k * n + to, 16), 16), :] = jnp.where(bits[k] == 1, sums[k], 0.0).astype(BF16)
            low = jnp.where(bits[k] == 1, 0.0, sums[k])
            back = low if back is None else back + low
        back_ref[pl.ds(pl.multiple_of(to, 16), 16), :] = back.astype(BF16)
    part2_b[...], part2_c[...] = shares(2, gb_ref, gc_ref, x_ref, d_ref, lam_ref, carry_ref, back_ref)


def grad_rest_kernel(gb_ref, gc_ref, x_ref, d_ref, lam_ref, carry_ref, back_ref, part0, part1, part3):
    for m, part in ((1, part1), (3, part3), (0, part0)):
        part[0], part[1] = shares(m, gb_ref, gc_ref, x_ref, d_ref, lam_ref, carry_ref, back_ref)


def output_kernel(mix_first, mix_middle, mix_last, x_ref, b_ref, c_ref, d_ref, lam_ref, carry_ref, back_ref, y_ref, dx_ref):
    tiles = [slice(at, at + TILE) for at in range(0, x_ref.shape[0], TILE)]
    mixes = {0: mix_first[...], 1: mix_middle[:TILE, : 2 * TILE], 2: mix_middle[TILE:, :], 3: mix_last[...]}
    for i, mine in enumerate(tiles):
        lam = lam_ref[mine, :]
        c_i = c_ref[mine, :].astype(F32)
        rising = jnp.concatenate([(c_i * lam[:, 11 + k : 12 + k]).astype(BF16) for k in range(5)], axis=1)
        total = dot_nn(rising, carry_ref[...])
        y_ref[mine, :] = (total + dot_nn(mixes[i], x_ref[: mine.stop, :])).astype(BF16)
    middle = slice(TILE, 3 * TILE)
    for i, mine in enumerate(tiles):
        total = dot_nn(b_ref[mine, :], back_ref[...]) + dot_tn(mix_last[:, mine], d_ref[tiles[3], :])
        if i < 2:
            total = total + dot_tn(mix_middle[:, mine], d_ref[middle, :])
        if i == 2:
            total = total + dot_tn(mix_middle[TILE:, mine], d_ref[mine, :])
        if i == 0:
            total = total + dot_tn(mix_first[...], d_ref[mine, :])
        dx_ref[mine, :] = total.astype(BF16)


def sum_kernel(part0, part1, part3, d_b_ref, d_c_ref):
    d_b_ref[...] = part0[0] + part1[0] + part3[0]
    d_c_ref[...] = part0[1] + part1[1] + part3[1]


def local(x_in, b_in, c_in, d_out, table, level_index):
    rows, width = x_in.shape
    n = b_in.shape[1]
    tie = lax.optimization_barrier
    half = ((2, n // 2, width), F32)
    table_rows = jnp.arange(table.shape[0], dtype=jnp.int32)
    chooser = (level_index[:, None] == table_rows[None, :]).astype(F32)
    lam = jnp.dot(chooser, table, precision=lax.Precision.HIGHEST)
    b_t, left = call(rows_kernel, (((n, rows), BF16), ((5 * n, rows), BF16)), [VMEM] * 2, LONG)(
        jnp.concatenate([b_in, c_in], axis=1), lam
    )
    far_send, far_keep, rest_send, near_keep = call(
        state_kernel,
        (half, half, ((4, n // 2, width), F32), half),
        [VMEM] * 4,
        2 * rows * width * n * 6,
    )(x_in, d_out, b_t, left)
    far, rest_send = tie((from_xor(far_send, CORE), rest_send))
    far = (far_keep + far).reshape(2, 4, n // 8, width)
    rest = from_xor(rest_send, CORE)
    near = (near_keep + rest[2:]).reshape(2, 4, n // 8, width)
    taken = [from_xor(far[:, m], Z[m]) for m in (2, 1, 3)]
    def local_part(kernel, mix, operands, flops):
        return call(kernel, ((mix, BF16), ((rows, n), F32), ((rows, n), F32)), [VMEM] * len(operands), flops)(*operands)

    x_tied, far, near = tie((x_in, far, near))
    mix_first, grad_b, grad_c = local_part(local_first, (TILE, TILE), (x_tied, b_in, c_in, d_out, lam), FIRST)
    total = far[:, 0]
    for part in taken:
        total = total + part
    near_later, total, grad_b = tie((near[1], total, grad_b))
    b3 = from_xor(total[0], X[1])
    b4 = from_xor(total[1], X[2]) + from_xor(total[1], X[3])
    r1, r3 = from_xor(near[0], Z[1]), from_xor(near[1], Z[3])
    r2 = from_xor(near_later, Z[2])
    r1, r3, b3, b4 = tie((r1, r3, b3, b4))
    b34 = jnp.stack([b3, b4])
    gathered = [from_xor(b34, Z[m]) for m in (1, 2, 3)]
    x_tied, b34 = tie((x_in, b34))
    mix_last, grad_b, grad_c = local_part(local_last, (TILE, rows), (grad_b, grad_c, x_tied, b_in, c_in, d_out, lam), LONG)
    mix_middle, grad_b, grad_c = local_part(
        local_middle, (2 * TILE, 3 * TILE), (grad_b, grad_c, x_tied, b_in, c_in, d_out, lam), LONG
    )
    near = jnp.stack([jnp.stack([r1[p ^ 1] for p in range(4)]), jnp.stack([r2[p ^ 2] + r3[p ^ 3] for p in range(4)])])
    near = near.reshape(2, n // 2, width)
    gathered, near, grad_b = tie((gathered, near, grad_b))
    far = jnp.stack([b34] + gathered, axis=1).reshape(2, n // 2, width)
    far_other, near_other = from_xor(far, CORE), from_xor(near, CORE)

    piece = ((2, rows // 4, n), F32)
    part2_b, part2_c, carry, back = call(
        grad_kernel,
        (((rows // 4, n), F32), ((rows // 4, n), F32), ((5 * n, width), BF16), ((n, width), BF16)),
        [VMEM] * 10,
        2 * rows * width * n * 6,
    )(rest, near, near_other, far, far_other, grad_b, grad_c, x_in, d_out, lam)
    part0, part1, part3 = call(
        grad_rest_kernel,
        (piece, piece, piece),
        [VMEM] * 7,
        2 * rows * width * n * 6,
    )(grad_b, grad_c, x_in, d_out, lam, carry, back)
    part3 = part3.at[0].add(from_xor(part2_b, 1, "head"))
    part1 = part1.at[1].add(from_xor(part2_c, 3, "head"))
    part1, part3 = from_xor(part1, 1, "head"), from_xor(part3, 3, "head")
    y_out, dx_out = call(
        output_kernel,
        (((rows, width), BF16), ((rows, width), BF16)),
        [VMEM] * 10,
        2 * rows * width * n * 6 + 2 * rows * rows * width,
    )(mix_first, mix_middle, mix_last, x_in, b_in, c_in, d_out, lam, carry, back)
    piece = ((rows // 4, n), F32)
    d_b, d_c = call(sum_kernel, (piece, piece), [VMEM] * 3, rows * n)(part0, part1, part3)
    return (y_out, dx_out, d_b, d_c)


def solution(mesh):
    return jax.shard_map(
        local,
        mesh=mesh,
        in_specs=(P("ctx", "head"), P("ctx", None), P("ctx", None), P("ctx", "head"), P(), P("ctx")),
        out_specs=(P("ctx", "head"), P("ctx", "head"), P(("ctx", "head"), None), P(("ctx", "head"), None)),
        check_vma=False,
    )
```

```python
import jax
import jax.numpy as jnp
from jax import lax
from jax.experimental import pallas as pl
from jax.experimental.pallas import tpu as pltpu
from jax.sharding import PartitionSpec as P

F32, BF16 = jnp.float32, jnp.bfloat16
CORE, Z, X = 1, (0, 2, 4, 6), (0, 8, 16, 24)
TILE = 256
VMEM = pl.BlockSpec(memory_space=pltpu.VMEM)
FIRST, LAST, LONG = 10**9, 10**9, 20 * 10**9


def from_xor(block, flip, axis="ctx"):
    route = [(i, i ^ flip) for i in range(lax.axis_size(axis))]
    return lax.ppermute(block, axis, route)


def dot_nt(a, b):
    return lax.dot_general(a, b, (((1,), (1,)), ((), ())), preferred_element_type=F32)


def dot_tn(a, b):
    return lax.dot_general(a, b, (((0,), (0,)), ((), ())), preferred_element_type=F32)


def dot_nn(a, b):
    return jnp.dot(a, b, preferred_element_type=F32)


def call(kernel, outs, in_specs, flops, scratch=(), mib=16):
    return pl.pallas_call(
        kernel,
        out_shape=tuple(jax.ShapeDtypeStruct(shape, dtype) for shape, dtype in outs),
        in_specs=in_specs,
        out_specs=tuple(VMEM for _ in outs),
        scratch_shapes=list(scratch),
        compiler_params=pltpu.CompilerParams(vmem_limit_bytes=mib << 20),
        cost_estimate=pl.CostEstimate(flops=flops, bytes_accessed=1 << 20, transcendentals=0),
    )


def own_bits():
    me = lax.axis_index("ctx")
    return [lax.shift_right_logical(me, k) & 1 for k in range(5)]


def row_mask(bits):
    return bits[0] * 64 + bits[2] * 32 + bits[1] * 16


def order_kernel(perm_ref):
    rows = lax.broadcasted_iota(jnp.int32, perm_ref.shape, 0)
    cols = lax.broadcasted_iota(jnp.int32, perm_ref.shape, 1)
    perm_ref[...] = (cols == (rows ^ row_mask(own_bits()))).astype(F32).astype(BF16)


def rows_kernel(bc_ref, lam_ref, perm_ref, b_t_ref, left):
    n = perm_ref.shape[0]
    perm = perm_ref[...]
    c_t = dot_nt(perm, bc_ref[:, n:])
    b_t_ref[...] = dot_nt(perm, bc_ref[:, :n]).astype(BF16)
    lam_t = lam_ref[...].T
    for k in range(5):
        left[k * n : (k + 1) * n, :] = (lam_t[11 + k : 12 + k, :] * c_t).astype(BF16)


def state_kernel(x_ref, d_ref, b_t_ref, left, far_send, far_keep, rest_send, near_keep):
    bits = own_bits()
    n = b_t_ref.shape[0]
    half = n // 2
    for at in range(0, x_ref.shape[1], TILE):
        here = slice(at, at + TILE)
        state = dot_nn(b_t_ref[...], x_ref[:, here])
        grads = dot_nn(left[...], d_ref[:, here])
        for k in range(5):
            value = jnp.where(bits[k] == 1, grads[k * n : (k + 1) * n], state)
            if k == 0:
                rest_send[0, :, here] = value[:half]
                rest_send[1, :, here] = value[half:]
            elif k < 3:
                near_keep[k - 1, :, here] = value[:half]
                rest_send[k + 1, :, here] = value[half:]
            else:
                far_keep[k - 3, :, here] = value[:half]
                far_send[k - 3, :, here] = value[half:]


def local_kernel(x_ref, b_ref, c_ref, d_ref, lam_ref, which, last, outs):
    mix_ref, grad_b_ref, grad_c_ref = outs
    tiles = [slice(at, at + TILE) for at in range(0, x_ref.shape[0], TILE)]
    rows = lax.broadcasted_iota(jnp.int32, (TILE, TILE), 0)
    cols = lax.broadcasted_iota(jnp.int32, (TILE, TILE), 1)
    gap = rows ^ cols
    if last is None:
        grad_b_ref[...] = jnp.zeros(grad_b_ref.shape, F32)
        grad_c_ref[...] = jnp.zeros(grad_c_ref.shape, F32)
    else:
        grad_b_ref[...] = last[0][...]
        grad_c_ref[...] = last[1][...]
    for i in which:
        mine = tiles[i]
        lam_i = lam_ref[mine, :]
        c_i = c_ref[mine, :]
        d_i = d_ref[mine, :]
        grad_c = None
        for j in range(i + 1):
            theirs = tiles[j]
            b_j = b_ref[theirs, :]
            if j == i:
                weight = jnp.broadcast_to(lam_i[:, 0:1], (TILE, TILE))
                for level in range(1, 9):
                    weight = jnp.where(gap >= (1 << (level - 1)), lam_i[:, level : level + 1], weight)
                weight = jnp.where(cols <= rows, weight, 0.0)
            else:
                level = 8 + (i ^ j).bit_length()
                weight = lam_i[:, level : level + 1]
            at = slice((i - which[0]) * TILE, (i - which[0] + 1) * TILE)
            mix_ref[at, theirs] = (dot_nt(c_i, b_j) * weight).astype(BF16)
            d_mix = (dot_nt(d_i, x_ref[theirs, :]) * weight).astype(BF16)
            term = dot_nn(d_mix, b_j)
            grad_c = term if grad_c is None else grad_c + term
            back = dot_tn(d_mix, c_i)
            grad_b_ref[theirs, :] += back
        grad_c_ref[mine, :] = grad_c


def local_first(*refs):
    local_kernel(*refs[:5], (0,), None, refs[5:])


def local_last(last_b, last_c, *refs):
    local_kernel(*refs[:5], (3,), (last_b, last_c), refs[5:])


def local_middle(last_b, last_c, *refs):
    local_kernel(*refs[:5], (1, 2), (last_b, last_c), refs[5:])


def shares(m, gb_ref, gc_ref, x_ref, d_ref, lam_ref, carry_ref, back_ref):
    n = gb_ref.shape[1]
    mine = pl.ds(pl.multiple_of((lax.axis_index("head") ^ m) * TILE, TILE), TILE)
    far_terms = dot_nt(d_ref[mine, :], carry_ref[...])
    lam = lam_ref[mine, :]
    grad_c = gc_ref[mine, :]
    for k in range(5):
        grad_c = grad_c + far_terms[:, k * n : (k + 1) * n] * lam[:, 11 + k : 12 + k]
    return gb_ref[mine, :] + dot_nt(x_ref[mine, :], back_ref[...]), grad_c


def grad_kernel(rest_ref, near_ref, near_other, far_ref, far_other, gb_ref, gc_ref, x_ref, d_ref, lam_ref, part2_b, part2_c, carry_ref, back_ref):
    bits = own_bits()
    mask = row_mask(bits) // 16
    n = gb_ref.shape[1]
    for p in range(8):
        to = (p ^ mask) * 16
        half, q = p // 4, slice(p % 4 * 16, p % 4 * 16 + 16)
        near, far = (near_ref, far_ref) if half == 0 else (near_other, far_other)
        sums = [rest_ref[1 - half, q, :], near[0, q, :], near[1, q, :], far[0, q, :], far[1, q, :]]
        back = None
        for k in range(5):
            carry_ref[pl.ds(pl.multiple_of(k * n + to, 16), 16), :] = jnp.where(bits[k] == 1, sums[k], 0.0).astype(BF16)
            low = jnp.where(bits[k] == 1, 0.0, sums[k])
            back = low if back is None else back + low
        back_ref[pl.ds(pl.multiple_of(to, 16), 16), :] = back.astype(BF16)
    part2_b[...], part2_c[...] = shares(2, gb_ref, gc_ref, x_ref, d_ref, lam_ref, carry_ref, back_ref)


def grad_rest_kernel(gb_ref, gc_ref, x_ref, d_ref, lam_ref, carry_ref, back_ref, part0, part1, part3):
    for m, part in ((1, part1), (3, part3), (0, part0)):
        part[0], part[1] = shares(m, gb_ref, gc_ref, x_ref, d_ref, lam_ref, carry_ref, back_ref)


def output_kernel(mix_first, mix_middle, mix_last, x_ref, b_ref, c_ref, d_ref, lam_ref, carry_ref, back_ref, y_ref, dx_ref):
    tiles = [slice(at, at + TILE) for at in range(0, x_ref.shape[0], TILE)]
    mixes = {0: mix_first[...], 1: mix_middle[:TILE, : 2 * TILE], 2: mix_middle[TILE:, :], 3: mix_last[...]}
    for i, mine in enumerate(tiles):
        lam = lam_ref[mine, :]
        c_i = c_ref[mine, :].astype(F32)
        rising = jnp.concatenate([(c_i * lam[:, 11 + k : 12 + k]).astype(BF16) for k in range(5)], axis=1)
        total = dot_nn(rising, carry_ref[...])
        y_ref[mine, :] = (total + dot_nn(mixes[i], x_ref[: mine.stop, :])).astype(BF16)
    middle = slice(TILE, 3 * TILE)
    for i, mine in enumerate(tiles):
        total = dot_nn(b_ref[mine, :], back_ref[...]) + dot_tn(mix_last[:, mine], d_ref[tiles[3], :])
        if i < 2:
            total = total + dot_tn(mix_middle[:, mine], d_ref[middle, :])
        if i == 2:
            total = total + dot_tn(mix_middle[TILE:, mine], d_ref[mine, :])
        if i == 0:
            total = total + dot_tn(mix_first[...], d_ref[mine, :])
        dx_ref[mine, :] = total.astype(BF16)


def sum_kernel(part0, part1, part3, d_b_ref, d_c_ref):
    d_b_ref[...] = part0[0] + part1[0] + part3[0]
    d_c_ref[...] = part0[1] + part1[1] + part3[1]


def local(x_in, b_in, c_in, d_out, table, level_index):
    rows, width = x_in.shape
    n = b_in.shape[1]
    tie = lax.optimization_barrier
    half = ((2, n // 2, width), F32)
    (perm,) = call(order_kernel, (((n, n), BF16),), [], LONG)()
    perm, level_index, b_first, c_first = tie((perm, level_index, b_in, c_in))
    table_rows = jnp.arange(table.shape[0], dtype=jnp.int32)
    chooser = (level_index[:, None] == table_rows[None, :]).astype(F32)
    lam = jnp.dot(chooser, table, precision=lax.Precision.HIGHEST)
    b_t, left = call(rows_kernel, (((n, rows), BF16), ((5 * n, rows), BF16)), [VMEM] * 3, 2 * rows * n * n)(
        jnp.concatenate([b_first, c_first], axis=1), lam, perm
    )
    far_send, far_keep, rest_send, near_keep = call(
        state_kernel,
        (half, half, ((4, n // 2, width), F32), half),
        [VMEM] * 4,
        2 * rows * width * n * 6,
    )(x_in, d_out, b_t, left)
    far, rest_send = tie((from_xor(far_send, CORE), rest_send))
    far = (far_keep + far).reshape(2, 4, n // 8, width)
    rest = from_xor(rest_send, CORE)
    near = (near_keep + rest[2:]).reshape(2, 4, n // 8, width)
    taken = [from_xor(far[:, m], Z[m]) for m in (2, 1, 3)]
    def local_part(kernel, mix, operands, flops):
        return call(kernel, ((mix, BF16), ((rows, n), F32), ((rows, n), F32)), [VMEM] * len(operands), flops)(*operands)

    x_tied, far, near = tie((x_in, far, near))
    mix_first, grad_b, grad_c = local_part(local_first, (TILE, TILE), (x_tied, b_in, c_in, d_out, lam), FIRST)
    total = far[:, 0]
    for part in taken:
        total = total + part
    near_later, total, grad_b = tie((near[1], total, grad_b))
    b3 = from_xor(total[0], X[1])
    b4 = from_xor(total[1], X[2]) + from_xor(total[1], X[3])
    r1, r3 = from_xor(near[0], Z[1]), from_xor(near[1], Z[3])
    r2 = from_xor(near_later, Z[2])
    r1, r3, b3, b4 = tie((r1, r3, b3, b4))
    b34 = jnp.stack([b3, b4])
    gathered = [from_xor(b34, Z[m]) for m in (1, 2, 3)]
    x_tied, b34 = tie((x_in, b34))
    mix_last, grad_b, grad_c = local_part(local_last, (TILE, rows), (grad_b, grad_c, x_tied, b_in, c_in, d_out, lam), LONG)
    mix_middle, grad_b, grad_c = local_part(
        local_middle, (2 * TILE, 3 * TILE), (grad_b, grad_c, x_tied, b_in, c_in, d_out, lam), LONG
    )
    near = jnp.stack([jnp.stack([r1[p ^ 1] for p in range(4)]), jnp.stack([r2[p ^ 2] + r3[p ^ 3] for p in range(4)])])
    near = near.reshape(2, n // 2, width)
    gathered, near, grad_b = tie((gathered, near, grad_b))
    far = jnp.stack([b34] + gathered, axis=1).reshape(2, n // 2, width)
    far_other, near_other = from_xor(far, CORE), from_xor(near, CORE)

    piece = ((2, rows // 4, n), F32)
    part2_b, part2_c, carry, back = call(
        grad_kernel,
        (((rows // 4, n), F32), ((rows // 4, n), F32), ((5 * n, width), BF16), ((n, width), BF16)),
        [VMEM] * 10,
        2 * rows * width * n * 6,
    )(rest, near, near_other, far, far_other, grad_b, grad_c, x_in, d_out, lam)
    part0, part1, part3 = call(
        grad_rest_kernel,
        (piece, piece, piece),
        [VMEM] * 7,
        2 * rows * width * n * 6,
    )(grad_b, grad_c, x_in, d_out, lam, carry, back)
    part3 = part3.at[0].add(from_xor(part2_b, 1, "head"))
    part1 = part1.at[1].add(from_xor(part2_c, 3, "head"))
    part1, part3 = from_xor(part1, 1, "head"), from_xor(part3, 3, "head")
    y_out, dx_out = call(
        output_kernel,
        (((rows, width), BF16), ((rows, width), BF16)),
        [VMEM] * 10,
        2 * rows * width * n * 6 + 2 * rows * rows * width,
    )(mix_first, mix_middle, mix_last, x_in, b_in, c_in, d_out, lam, carry, back)
    piece = ((rows // 4, n), F32)
    d_b, d_c = call(sum_kernel, (piece, piece), [VMEM] * 3, rows * n)(part0, part1, part3)
    return (y_out, dx_out, d_b, d_c)


def solution(mesh):
    return jax.shard_map(
        local,
        mesh=mesh,
        in_specs=(P("ctx", "head"), P("ctx", None), P("ctx", None), P("ctx", "head"), P(), P("ctx")),
        out_specs=(P("ctx", "head"), P("ctx", "head"), P(("ctx", "head"), None), P(("ctx", "head"), None)),
        check_vma=False,
    )
```

```python
import jax
import jax.numpy as jnp
from jax import lax
from jax.experimental import pallas as pl
from jax.experimental.pallas import tpu as pltpu
from jax.sharding import PartitionSpec as P

F32, BF16 = jnp.float32, jnp.bfloat16
CORE, Z, X = 1, (0, 2, 4, 6), (0, 8, 16, 24)
TILE = 256
VMEM = pl.BlockSpec(memory_space=pltpu.VMEM)
FIRST, LAST, LONG = 10**9, 10**9, 20 * 10**9


def from_xor(block, flip, axis="ctx"):
    route = [(i, i ^ flip) for i in range(lax.axis_size(axis))]
    return lax.ppermute(block, axis, route)


def dot_nt(a, b):
    return lax.dot_general(a, b, (((1,), (1,)), ((), ())), preferred_element_type=F32)


def dot_tn(a, b):
    return lax.dot_general(a, b, (((0,), (0,)), ((), ())), preferred_element_type=F32)


def dot_nn(a, b):
    return jnp.dot(a, b, preferred_element_type=F32)


def call(kernel, outs, in_specs, flops, scratch=(), mib=16):
    return pl.pallas_call(
        kernel,
        out_shape=tuple(jax.ShapeDtypeStruct(shape, dtype) for shape, dtype in outs),
        in_specs=in_specs,
        out_specs=tuple(VMEM for _ in outs),
        scratch_shapes=list(scratch),
        compiler_params=pltpu.CompilerParams(vmem_limit_bytes=mib << 20),
        cost_estimate=pl.CostEstimate(flops=flops, bytes_accessed=1 << 20, transcendentals=0),
    )


def own_bits():
    me = lax.axis_index("ctx")
    return [lax.shift_right_logical(me, k) & 1 for k in range(5)]


def row_mask(bits):
    return bits[0] * 64 + bits[2] * 32 + bits[1] * 16


def order_kernel(perm_ref):
    rows = lax.broadcasted_iota(jnp.int32, perm_ref.shape, 0)
    cols = lax.broadcasted_iota(jnp.int32, perm_ref.shape, 1)
    perm_ref[...] = (cols == (rows ^ row_mask(own_bits()))).astype(F32).astype(BF16)


def rows_kernel(bc_ref, lam_ref, perm_ref, b_t_ref, left):
    n = perm_ref.shape[0]
    perm = perm_ref[...]
    c_t = dot_nt(perm, bc_ref[:, n:])
    b_t_ref[...] = dot_nt(perm, bc_ref[:, :n]).astype(BF16)
    lam_t = lam_ref[...].T
    for k in range(5):
        left[k * n : (k + 1) * n, :] = (lam_t[11 + k : 12 + k, :] * c_t).astype(BF16)


def slots(levels, x_ref, d_ref, b_t_ref, left, here):
    bits = own_bits()
    n = b_t_ref.shape[0]
    state = dot_nn(b_t_ref[...], x_ref[:, here])
    grads = dot_nn(left[levels[0] * n : (levels[-1] + 1) * n, :], d_ref[:, here])
    return [jnp.where(bits[k] == 1, grads[i * n : (i + 1) * n], state) for i, k in enumerate(levels)]


def far_kernel(x_ref, d_ref, b_t_ref, left, far_send, far_keep):
    half = b_t_ref.shape[0] // 2
    for at in range(0, x_ref.shape[1], TILE):
        here = slice(at, at + TILE)
        for k, value in enumerate(slots((3, 4), x_ref, d_ref, b_t_ref, left, here)):
            far_keep[k, :, here] = value[:half]
            far_send[k, :, here] = value[half:]


def rest_kernel(x_ref, d_ref, b_t_ref, left, rest_send, near_keep):
    half = b_t_ref.shape[0] // 2
    for at in range(0, x_ref.shape[1], TILE):
        here = slice(at, at + TILE)
        values = slots((0, 1, 2), x_ref, d_ref, b_t_ref, left, here)
        rest_send[0, :, here] = values[0][:half]
        rest_send[1, :, here] = values[0][half:]
        for k in (1, 2):
            near_keep[k - 1, :, here] = values[k][:half]
            rest_send[k + 1, :, here] = values[k][half:]


def local_kernel(x_ref, b_ref, c_ref, d_ref, lam_ref, which, last, outs):
    mix_ref, grad_b_ref, grad_c_ref = outs
    tiles = [slice(at, at + TILE) for at in range(0, x_ref.shape[0], TILE)]
    rows = lax.broadcasted_iota(jnp.int32, (TILE, TILE), 0)
    cols = lax.broadcasted_iota(jnp.int32, (TILE, TILE), 1)
    gap = rows ^ cols
    if last is None:
        grad_b_ref[...] = jnp.zeros(grad_b_ref.shape, F32)
        grad_c_ref[...] = jnp.zeros(grad_c_ref.shape, F32)
    else:
        grad_b_ref[...] = last[0][...]
        grad_c_ref[...] = last[1][...]
    for i in which:
        mine = tiles[i]
        lam_i = lam_ref[mine, :]
        c_i = c_ref[mine, :]
        d_i = d_ref[mine, :]
        grad_c = None
        for j in range(i + 1):
            theirs = tiles[j]
            b_j = b_ref[theirs, :]
            if j == i:
                weight = jnp.broadcast_to(lam_i[:, 0:1], (TILE, TILE))
                for level in range(1, 9):
                    weight = jnp.where(gap >= (1 << (level - 1)), lam_i[:, level : level + 1], weight)
                weight = jnp.where(cols <= rows, weight, 0.0)
            else:
                level = 8 + (i ^ j).bit_length()
                weight = lam_i[:, level : level + 1]
            at = slice((i - which[0]) * TILE, (i - which[0] + 1) * TILE)
            mix_ref[at, theirs] = (dot_nt(c_i, b_j) * weight).astype(BF16)
            d_mix = (dot_nt(d_i, x_ref[theirs, :]) * weight).astype(BF16)
            term = dot_nn(d_mix, b_j)
            grad_c = term if grad_c is None else grad_c + term
            back = dot_tn(d_mix, c_i)
            grad_b_ref[theirs, :] += back
        grad_c_ref[mine, :] = grad_c


def local_first(*refs):
    local_kernel(*refs[:5], (0,), None, refs[5:])


def local_last(last_b, last_c, *refs):
    local_kernel(*refs[:5], (3,), (last_b, last_c), refs[5:])


def local_middle(last_b, last_c, *refs):
    local_kernel(*refs[:5], (1, 2), (last_b, last_c), refs[5:])


def shares(m, gb_ref, gc_ref, x_ref, d_ref, lam_ref, carry_ref, back_ref):
    n = gb_ref.shape[1]
    mine = pl.ds(pl.multiple_of((lax.axis_index("head") ^ m) * TILE, TILE), TILE)
    far_terms = dot_nt(d_ref[mine, :], carry_ref[...])
    lam = lam_ref[mine, :]
    grad_c = gc_ref[mine, :]
    for k in range(5):
        grad_c = grad_c + far_terms[:, k * n : (k + 1) * n] * lam[:, 11 + k : 12 + k]
    return gb_ref[mine, :] + dot_nt(x_ref[mine, :], back_ref[...]), grad_c


def grad_kernel(rest_ref, near_ref, near_other, far_ref, far_other, gb_ref, gc_ref, x_ref, d_ref, lam_ref, part2_b, part2_c, carry_ref, back_ref):
    bits = own_bits()
    mask = row_mask(bits) // 16
    n = gb_ref.shape[1]
    for p in range(8):
        to = (p ^ mask) * 16
        half, q = p // 4, slice(p % 4 * 16, p % 4 * 16 + 16)
        near, far = (near_ref, far_ref) if half == 0 else (near_other, far_other)
        sums = [rest_ref[1 - half, q, :], near[0, q, :], near[1, q, :], far[0, q, :], far[1, q, :]]
        back = None
        for k in range(5):
            carry_ref[pl.ds(pl.multiple_of(k * n + to, 16), 16), :] = jnp.where(bits[k] == 1, sums[k], 0.0).astype(BF16)
            low = jnp.where(bits[k] == 1, 0.0, sums[k])
            back = low if back is None else back + low
        back_ref[pl.ds(pl.multiple_of(to, 16), 16), :] = back.astype(BF16)
    part2_b[...], part2_c[...] = shares(2, gb_ref, gc_ref, x_ref, d_ref, lam_ref, carry_ref, back_ref)


def grad_rest_kernel(gb_ref, gc_ref, x_ref, d_ref, lam_ref, carry_ref, back_ref, part0, part1, part3):
    for m, part in ((1, part1), (3, part3), (0, part0)):
        part[0], part[1] = shares(m, gb_ref, gc_ref, x_ref, d_ref, lam_ref, carry_ref, back_ref)


def output_kernel(mix_first, mix_middle, mix_last, x_ref, b_ref, c_ref, d_ref, lam_ref, carry_ref, back_ref, y_ref, dx_ref):
    tiles = [slice(at, at + TILE) for at in range(0, x_ref.shape[0], TILE)]
    mixes = {0: mix_first[...], 1: mix_middle[:TILE, : 2 * TILE], 2: mix_middle[TILE:, :], 3: mix_last[...]}
    for i, mine in enumerate(tiles):
        lam = lam_ref[mine, :]
        c_i = c_ref[mine, :].astype(F32)
        rising = jnp.concatenate([(c_i * lam[:, 11 + k : 12 + k]).astype(BF16) for k in range(5)], axis=1)
        total = dot_nn(rising, carry_ref[...])
        y_ref[mine, :] = (total + dot_nn(mixes[i], x_ref[: mine.stop, :])).astype(BF16)
    middle = slice(TILE, 3 * TILE)
    for i, mine in enumerate(tiles):
        total = dot_nn(b_ref[mine, :], back_ref[...]) + dot_tn(mix_last[:, mine], d_ref[tiles[3], :])
        if i < 2:
            total = total + dot_tn(mix_middle[:, mine], d_ref[middle, :])
        if i == 2:
            total = total + dot_tn(mix_middle[TILE:, mine], d_ref[mine, :])
        if i == 0:
            total = total + dot_tn(mix_first[...], d_ref[mine, :])
        dx_ref[mine, :] = total.astype(BF16)


def sum_kernel(part0, part1, part3, d_b_ref, d_c_ref):
    d_b_ref[...] = part0[0] + part1[0] + part3[0]
    d_c_ref[...] = part0[1] + part1[1] + part3[1]


def local(x_in, b_in, c_in, d_out, table, level_index):
    rows, width = x_in.shape
    n = b_in.shape[1]
    tie = lax.optimization_barrier
    half = ((2, n // 2, width), F32)
    (perm,) = call(order_kernel, (((n, n), BF16),), [], LONG)()
    perm, level_index, b_first, c_first = tie((perm, level_index, b_in, c_in))
    table_rows = jnp.arange(table.shape[0], dtype=jnp.int32)
    chooser = (level_index[:, None] == table_rows[None, :]).astype(F32)
    lam = jnp.dot(chooser, table, precision=lax.Precision.HIGHEST)
    b_t, left = call(rows_kernel, (((n, rows), BF16), ((5 * n, rows), BF16)), [VMEM] * 3, 2 * rows * n * n)(
        jnp.concatenate([b_first, c_first], axis=1), lam, perm
    )
    far_send, far_keep = call(far_kernel, (half, half), [VMEM] * 4, 2 * rows * width * n * 3)(x_in, d_out, b_t, left)
    far_send, b_t = tie((far_send, b_t))
    rest_send, near_keep = call(
        rest_kernel, (((4, n // 2, width), F32), half), [VMEM] * 4, 2 * rows * width * n * 4
    )(x_in, d_out, b_t, left)
    far, rest_send = tie((from_xor(far_send, CORE), rest_send))
    far = (far_keep + far).reshape(2, 4, n // 8, width)
    rest = from_xor(rest_send, CORE)
    near = (near_keep + rest[2:]).reshape(2, 4, n // 8, width)
    taken = [from_xor(far[:, m], Z[m]) for m in (2, 1, 3)]
    def local_part(kernel, mix, operands, flops):
        return call(kernel, ((mix, BF16), ((rows, n), F32), ((rows, n), F32)), [VMEM] * len(operands), flops)(*operands)

    x_tied, far, near = tie((x_in, far, near))
    mix_first, grad_b, grad_c = local_part(local_first, (TILE, TILE), (x_tied, b_in, c_in, d_out, lam), FIRST)
    total = far[:, 0]
    for part in taken:
        total = total + part
    near_later, total, grad_b = tie((near[1], total, grad_b))
    b3 = from_xor(total[0], X[1])
    b4 = from_xor(total[1], X[2]) + from_xor(total[1], X[3])
    r1, r3 = from_xor(near[0], Z[1]), from_xor(near[1], Z[3])
    r2 = from_xor(near_later, Z[2])
    r1, r3, b3, b4 = tie((r1, r3, b3, b4))
    b34 = jnp.stack([b3, b4])
    gathered = [from_xor(b34, Z[m]) for m in (1, 2, 3)]
    x_tied, b34 = tie((x_in, b34))
    mix_last, grad_b, grad_c = local_part(local_last, (TILE, rows), (grad_b, grad_c, x_tied, b_in, c_in, d_out, lam), LONG)
    mix_middle, grad_b, grad_c = local_part(
        local_middle, (2 * TILE, 3 * TILE), (grad_b, grad_c, x_tied, b_in, c_in, d_out, lam), LONG
    )
    near = jnp.stack([jnp.stack([r1[p ^ 1] for p in range(4)]), jnp.stack([r2[p ^ 2] + r3[p ^ 3] for p in range(4)])])
    near = near.reshape(2, n // 2, width)
    gathered, near, grad_b = tie((gathered, near, grad_b))
    far = jnp.stack([b34] + gathered, axis=1).reshape(2, n // 2, width)
    far_other, near_other = from_xor(far, CORE), from_xor(near, CORE)

    piece = ((2, rows // 4, n), F32)
    part2_b, part2_c, carry, back = call(
        grad_kernel,
        (((rows // 4, n), F32), ((rows // 4, n), F32), ((5 * n, width), BF16), ((n, width), BF16)),
        [VMEM] * 10,
        2 * rows * width * n * 6,
    )(rest, near, near_other, far, far_other, grad_b, grad_c, x_in, d_out, lam)
    part0, part1, part3 = call(
        grad_rest_kernel,
        (piece, piece, piece),
        [VMEM] * 7,
        2 * rows * width * n * 6,
    )(grad_b, grad_c, x_in, d_out, lam, carry, back)
    part3 = part3.at[0].add(from_xor(part2_b, 1, "head"))
    part1 = part1.at[1].add(from_xor(part2_c, 3, "head"))
    part1, part3 = from_xor(part1, 1, "head"), from_xor(part3, 3, "head")
    y_out, dx_out = call(
        output_kernel,
        (((rows, width), BF16), ((rows, width), BF16)),
        [VMEM] * 10,
        2 * rows * width * n * 6 + 2 * rows * rows * width,
    )(mix_first, mix_middle, mix_last, x_in, b_in, c_in, d_out, lam, carry, back)
    piece = ((rows // 4, n), F32)
    d_b, d_c = call(sum_kernel, (piece, piece), [VMEM] * 3, rows * n)(part0, part1, part3)
    return (y_out, dx_out, d_b, d_c)


def solution(mesh):
    return jax.shard_map(
        local,
        mesh=mesh,
        in_specs=(P("ctx", "head"), P("ctx", None), P("ctx", None), P("ctx", "head"), P(), P("ctx")),
        out_specs=(P("ctx", "head"), P("ctx", "head"), P(("ctx", "head"), None), P(("ctx", "head"), None)),
        check_vma=False,
    )
```

```python
import jax
import jax.numpy as jnp
from jax import lax
from jax.experimental import pallas as pl
from jax.experimental.pallas import tpu as pltpu
from jax.sharding import PartitionSpec as P

F32, BF16 = jnp.float32, jnp.bfloat16
CORE, Z, X = 1, (0, 2, 4, 6), (0, 8, 16, 24)
TILE = 256
VMEM = pl.BlockSpec(memory_space=pltpu.VMEM)
FIRST, LAST, LONG = 10**9, 10**9, 20 * 10**9


def from_xor(block, flip, axis="ctx"):
    route = [(i, i ^ flip) for i in range(lax.axis_size(axis))]
    return lax.ppermute(block, axis, route)


def dot_nt(a, b):
    return lax.dot_general(a, b, (((1,), (1,)), ((), ())), preferred_element_type=F32)


def dot_tn(a, b):
    return lax.dot_general(a, b, (((0,), (0,)), ((), ())), preferred_element_type=F32)


def dot_nn(a, b):
    return jnp.dot(a, b, preferred_element_type=F32)


def call(kernel, outs, in_specs, flops, scratch=(), mib=16):
    return pl.pallas_call(
        kernel,
        out_shape=tuple(jax.ShapeDtypeStruct(shape, dtype) for shape, dtype in outs),
        in_specs=in_specs,
        out_specs=tuple(VMEM for _ in outs),
        scratch_shapes=list(scratch),
        compiler_params=pltpu.CompilerParams(vmem_limit_bytes=mib << 20),
        cost_estimate=pl.CostEstimate(flops=flops, bytes_accessed=1 << 20, transcendentals=0),
    )


def own_bits():
    me = lax.axis_index("ctx")
    return [lax.shift_right_logical(me, k) & 1 for k in range(5)]


def row_mask(bits):
    return bits[0] * 64 + bits[2] * 32 + bits[1] * 16


def order_kernel(perm_ref):
    rows = lax.broadcasted_iota(jnp.int32, perm_ref.shape, 0)
    cols = lax.broadcasted_iota(jnp.int32, perm_ref.shape, 1)
    perm_ref[...] = (cols == (rows ^ row_mask(own_bits()))).astype(F32).astype(BF16)


def rows_kernel(bc_ref, lam_ref, perm_ref, b_t_ref, left):
    n = perm_ref.shape[0]
    perm = perm_ref[...]
    c_t = dot_nt(perm, bc_ref[:, n:])
    b_t_ref[...] = dot_nt(perm, bc_ref[:, :n]).astype(BF16)
    lam_t = lam_ref[...].T
    for k in range(5):
        left[k * n : (k + 1) * n, :] = (lam_t[11 + k : 12 + k, :] * c_t).astype(BF16)


def slots(levels, x_ref, d_ref, b_t_ref, left, here):
    bits = own_bits()
    n = b_t_ref.shape[0]
    state = dot_nn(b_t_ref[...], x_ref[:, here])
    grads = dot_nn(left[levels[0] * n : (levels[-1] + 1) * n, :], d_ref[:, here])
    return [jnp.where(bits[k] == 1, grads[i * n : (i + 1) * n], state) for i, k in enumerate(levels)]


def far_kernel(x_ref, d_ref, b_t_ref, left, far_send, far_keep):
    half = b_t_ref.shape[0] // 2
    for at in range(0, x_ref.shape[1], TILE):
        here = slice(at, at + TILE)
        for k, value in enumerate(slots((3, 4), x_ref, d_ref, b_t_ref, left, here)):
            far_keep[k, :, here] = value[:half]
            far_send[k, :, here] = value[half:]


def rest_kernel(x_ref, d_ref, b_t_ref, left, rest_send, near_keep):
    half = b_t_ref.shape[0] // 2
    for at in range(0, x_ref.shape[1], TILE):
        here = slice(at, at + TILE)
        values = slots((0, 1, 2), x_ref, d_ref, b_t_ref, left, here)
        rest_send[0, :, here] = values[0][:half]
        rest_send[1, :, here] = values[0][half:]
        for k in (1, 2):
            near_keep[k - 1, :, here] = values[k][:half]
            rest_send[k + 1, :, here] = values[k][half:]


def local_kernel(x_ref, b_ref, c_ref, d_ref, lam_ref, which, last, outs):
    mix_ref, grad_b_ref, grad_c_ref = outs
    tiles = [slice(at, at + TILE) for at in range(0, x_ref.shape[0], TILE)]
    rows = lax.broadcasted_iota(jnp.int32, (TILE, TILE), 0)
    cols = lax.broadcasted_iota(jnp.int32, (TILE, TILE), 1)
    gap = rows ^ cols
    if last is None:
        grad_b_ref[...] = jnp.zeros(grad_b_ref.shape, F32)
        grad_c_ref[...] = jnp.zeros(grad_c_ref.shape, F32)
    else:
        grad_b_ref[...] = last[0][...]
        grad_c_ref[...] = last[1][...]
    for i in which:
        mine = tiles[i]
        lam_i = lam_ref[mine, :]
        c_i = c_ref[mine, :]
        d_i = d_ref[mine, :]
        grad_c = None
        for j in range(i + 1):
            theirs = tiles[j]
            b_j = b_ref[theirs, :]
            if j == i:
                weight = jnp.broadcast_to(lam_i[:, 0:1], (TILE, TILE))
                for level in range(1, 9):
                    weight = jnp.where(gap >= (1 << (level - 1)), lam_i[:, level : level + 1], weight)
                weight = jnp.where(cols <= rows, weight, 0.0)
            else:
                level = 8 + (i ^ j).bit_length()
                weight = lam_i[:, level : level + 1]
            at = slice((i - which[0]) * TILE, (i - which[0] + 1) * TILE)
            mix_ref[at, theirs] = (dot_nt(c_i, b_j) * weight).astype(BF16)
            d_mix = (dot_nt(d_i, x_ref[theirs, :]) * weight).astype(BF16)
            term = dot_nn(d_mix, b_j)
            grad_c = term if grad_c is None else grad_c + term
            back = dot_tn(d_mix, c_i)
            grad_b_ref[theirs, :] += back
        grad_c_ref[mine, :] = grad_c


def local_first(*refs):
    local_kernel(*refs[:5], (0,), None, refs[5:])


def local_last(last_b, last_c, *refs):
    local_kernel(*refs[:5], (3,), (last_b, last_c), refs[5:])


def local_middle(last_b, last_c, *refs):
    local_kernel(*refs[:5], (1, 2), (last_b, last_c), refs[5:])


def shares(m, gb_ref, gc_ref, x_ref, d_ref, lam_ref, carry_ref, back_ref):
    n = gb_ref.shape[1]
    mine = pl.ds(pl.multiple_of((lax.axis_index("head") ^ m) * TILE, TILE), TILE)
    far_terms = dot_nt(d_ref[mine, :], carry_ref[...])
    lam = lam_ref[mine, :]
    grad_c = gc_ref[mine, :]
    for k in range(5):
        grad_c = grad_c + far_terms[:, k * n : (k + 1) * n] * lam[:, 11 + k : 12 + k]
    return gb_ref[mine, :] + dot_nt(x_ref[mine, :], back_ref[...]), grad_c


def grad_kernel(rest_ref, own_ref, other_ref, gb_ref, gc_ref, x_ref, d_ref, lam_ref, part2_b, part2_c, carry_ref, back_ref):
    bits = own_bits()
    mask = row_mask(bits) // 16
    n = gb_ref.shape[1]
    for p in range(8):
        to = (p ^ mask) * 16
        half, q = p // 4, slice(p % 4 * 16, p % 4 * 16 + 16)
        got = own_ref if half == 0 else other_ref
        sums = [rest_ref[1 - half, q, :], got[0, q, :], got[1, q, :], got[2, q, :], got[3, q, :]]
        back = None
        for k in range(5):
            carry_ref[pl.ds(pl.multiple_of(k * n + to, 16), 16), :] = jnp.where(bits[k] == 1, sums[k], 0.0).astype(BF16)
            low = jnp.where(bits[k] == 1, 0.0, sums[k])
            back = low if back is None else back + low
        back_ref[pl.ds(pl.multiple_of(to, 16), 16), :] = back.astype(BF16)
    part2_b[...], part2_c[...] = shares(2, gb_ref, gc_ref, x_ref, d_ref, lam_ref, carry_ref, back_ref)


def grad_rest_kernel(gb_ref, gc_ref, x_ref, d_ref, lam_ref, carry_ref, back_ref, part0, part1, part3):
    for m, part in ((1, part1), (3, part3), (0, part0)):
        part[0], part[1] = shares(m, gb_ref, gc_ref, x_ref, d_ref, lam_ref, carry_ref, back_ref)


def output_kernel(mix_first, mix_middle, mix_last, x_ref, b_ref, c_ref, d_ref, lam_ref, carry_ref, back_ref, y_ref, dx_ref):
    tiles = [slice(at, at + TILE) for at in range(0, x_ref.shape[0], TILE)]
    mixes = {0: mix_first[...], 1: mix_middle[:TILE, : 2 * TILE], 2: mix_middle[TILE:, :], 3: mix_last[...]}
    for i, mine in enumerate(tiles):
        lam = lam_ref[mine, :]
        c_i = c_ref[mine, :].astype(F32)
        rising = jnp.concatenate([(c_i * lam[:, 11 + k : 12 + k]).astype(BF16) for k in range(5)], axis=1)
        total = dot_nn(rising, carry_ref[...])
        y_ref[mine, :] = (total + dot_nn(mixes[i], x_ref[: mine.stop, :])).astype(BF16)
    middle = slice(TILE, 3 * TILE)
    for i, mine in enumerate(tiles):
        total = dot_nn(b_ref[mine, :], back_ref[...]) + dot_tn(mix_last[:, mine], d_ref[tiles[3], :])
        if i < 2:
            total = total + dot_tn(mix_middle[:, mine], d_ref[middle, :])
        if i == 2:
            total = total + dot_tn(mix_middle[TILE:, mine], d_ref[mine, :])
        if i == 0:
            total = total + dot_tn(mix_first[...], d_ref[mine, :])
        dx_ref[mine, :] = total.astype(BF16)


def sum_kernel(part0, part1, part3, d_b_ref, d_c_ref):
    d_b_ref[...] = part0[0] + part1[0] + part3[0]
    d_c_ref[...] = part0[1] + part1[1] + part3[1]


def local(x_in, b_in, c_in, d_out, table, level_index):
    rows, width = x_in.shape
    n = b_in.shape[1]
    tie = lax.optimization_barrier
    half = ((2, n // 2, width), F32)
    (perm,) = call(order_kernel, (((n, n), BF16),), [], LONG)()
    perm, level_index, b_first, c_first = tie((perm, level_index, b_in, c_in))
    table_rows = jnp.arange(table.shape[0], dtype=jnp.int32)
    chooser = (level_index[:, None] == table_rows[None, :]).astype(F32)
    lam = jnp.dot(chooser, table, precision=lax.Precision.HIGHEST)
    b_t, left = call(rows_kernel, (((n, rows), BF16), ((5 * n, rows), BF16)), [VMEM] * 3, 2 * rows * n * n)(
        jnp.concatenate([b_first, c_first], axis=1), lam, perm
    )
    far_send, far_keep = call(far_kernel, (half, half), [VMEM] * 4, 2 * rows * width * n * 3)(x_in, d_out, b_t, left)
    far_send, b_t = tie((far_send, b_t))
    rest_send, near_keep = call(
        rest_kernel, (((4, n // 2, width), F32), half), [VMEM] * 4, 2 * rows * width * n * 4
    )(x_in, d_out, b_t, left)
    far, rest_send = tie((from_xor(far_send, CORE), rest_send))
    far = (far_keep + far).reshape(2, 4, n // 8, width)
    rest = from_xor(rest_send, CORE)
    near = (near_keep + rest[2:]).reshape(2, 4, n // 8, width)
    taken = [from_xor(far[:, m], Z[m]) for m in (2, 1, 3)]
    def local_part(kernel, mix, operands, flops):
        return call(kernel, ((mix, BF16), ((rows, n), F32), ((rows, n), F32)), [VMEM] * len(operands), flops)(*operands)

    x_tied, far, near = tie((x_in, far, near))
    mix_first, grad_b, grad_c = local_part(local_first, (TILE, TILE), (x_tied, b_in, c_in, d_out, lam), FIRST)
    total = far[:, 0]
    for part in taken:
        total = total + part
    near_later, total, grad_b = tie((near[1], total, grad_b))
    b3 = from_xor(total[0], X[1])
    b4 = from_xor(total[1], X[2]) + from_xor(total[1], X[3])
    r1, r3 = from_xor(near[0], Z[1]), from_xor(near[1], Z[3])
    r2 = from_xor(near_later, Z[2])
    r1, r3, b3, b4 = tie((r1, r3, b3, b4))
    b34 = jnp.stack([b3, b4])
    gathered = [from_xor(b34, Z[m]) for m in (1, 2, 3)]
    x_tied, b34 = tie((x_in, b34))
    mix_last, grad_b, grad_c = local_part(local_last, (TILE, rows), (grad_b, grad_c, x_tied, b_in, c_in, d_out, lam), LONG)
    mix_middle, grad_b, grad_c = local_part(
        local_middle, (2 * TILE, 3 * TILE), (grad_b, grad_c, x_tied, b_in, c_in, d_out, lam), LONG
    )
    near = jnp.stack([jnp.stack([r1[p ^ 1] for p in range(4)]), jnp.stack([r2[p ^ 2] + r3[p ^ 3] for p in range(4)])])
    near = near.reshape(2, n // 2, width)
    gathered, near, grad_b = tie((gathered, near, grad_b))
    far = jnp.stack([b34] + gathered, axis=1).reshape(2, n // 2, width)
    own = jnp.concatenate([near, far])
    other = from_xor(own, CORE)

    piece = ((2, rows // 4, n), F32)
    part2_b, part2_c, carry, back = call(
        grad_kernel,
        (((rows // 4, n), F32), ((rows // 4, n), F32), ((5 * n, width), BF16), ((n, width), BF16)),
        [VMEM] * 8,
        2 * rows * width * n * 6,
    )(rest, own, other, grad_b, grad_c, x_in, d_out, lam)
    part0, part1, part3 = call(
        grad_rest_kernel,
        (piece, piece, piece),
        [VMEM] * 7,
        2 * rows * width * n * 6,
    )(grad_b, grad_c, x_in, d_out, lam, carry, back)
    part3 = part3.at[0].add(from_xor(part2_b, 1, "head"))
    part1 = part1.at[1].add(from_xor(part2_c, 3, "head"))
    part1, part3 = from_xor(part1, 1, "head"), from_xor(part3, 3, "head")
    y_out, dx_out = call(
        output_kernel,
        (((rows, width), BF16), ((rows, width), BF16)),
        [VMEM] * 10,
        2 * rows * width * n * 6 + 2 * rows * rows * width,
    )(mix_first, mix_middle, mix_last, x_in, b_in, c_in, d_out, lam, carry, back)
    piece = ((rows // 4, n), F32)
    d_b, d_c = call(sum_kernel, (piece, piece), [VMEM] * 3, rows * n)(part0, part1, part3)
    return (y_out, dx_out, d_b, d_c)


def solution(mesh):
    return jax.shard_map(
        local,
        mesh=mesh,
        in_specs=(P("ctx", "head"), P("ctx", None), P("ctx", None), P("ctx", "head"), P(), P("ctx")),
        out_specs=(P("ctx", "head"), P("ctx", "head"), P(("ctx", "head"), None), P(("ctx", "head"), None)),
        check_vma=False,
    )
```
